32 devices in a mesh: section: 4 (over z), expert: 8 (over y, x, core).
Axes of the slice: x: 2, y: 2, z: 4, core: 2. Of those that a mesh axis runs over, the one named last changes fastest.
Arguments:
- grad_out: bfloat16 [1024, 4096], P('expert', 'section'), may hold values from -6 to 6
- probs: float32 [1024, 8], P('expert'), may hold values from 0.05 to 0.4
- expert_ids: int32 [1024, 8], P('expert'), may hold values from 0 to 15, all different within a row; in each aligned block of 128 rows (0 to 127, 128 to 255, ...) at most 96 rows name the same one
- w_gate: bfloat16 [16, 1536, 4096], P('expert', 'section'), may hold values from -0.09375 to 0.09375
- w_up: bfloat16 [16, 1536, 4096], P('expert', 'section'), may hold values from -0.09375 to 0.09375
- w_down: bfloat16 [16, 1536, 4096], P('expert', 'section'), may hold values from -0.15625 to 0.15625
- saved_gate: bfloat16 [16, 1536, 768], P('expert', 'section'), may hold values from -3 to 3
- saved_up: bfloat16 [16, 1536, 768], P('expert', 'section'), may hold values from -3 to 3
Outputs:
- grad_in: bfloat16 [1024, 4096], P('expert', 'section')
- grad_probs: bfloat16 [1024, 8], P('expert')
The draws below stay inside these ranges and needn't reach their ends.
Inputs may be any that keep to these rules, and one draw needn't show every extreme that they name: `expert_ids`: each token names 8 different experts. Within the tokens of one index of expert (aligned blocks of 128 tokens) no expert is named more than 96 times, a bound that some block reaches.
All inputs are finite; a program needn't handle non-finite values.
Results may differ from the reference program's by a relative error of at most 0.015.
Values may be sent and summed in bfloat16 or wider, within the bound.
No kernel may reach another device: no remote copies, remote signals or barrier semaphores. Data moves between devices by JAX's collectives and lax.ppermute only.
A program may use at most 128 MiB of HBM per device.

```python
import math
import jax
import jax.numpy as jnp
import numpy as np
from jax import lax

D = 4096
FF = 1536
TOPK = 8
TOK_DEV = 128
EXPERTS = 16
CAP = 96
SLOTS = 768
TOKENS = 1024
N_SECTION = 4
N_EXPERT = 8


def steps_of(rng, shape, cuts, smallest, largest):
    gain = 1.0
    for dim, parts in cuts:
        heights = jax.random.uniform(jax.random.fold_in(jax.random.fold_in(rng, 6), dim), (parts,), jnp.float32, smallest / len(cuts), largest / len(cuts))
        gain = gain * jnp.repeat(jnp.exp(heights), shape[dim] // parts).reshape((-1,) + (1,) * (len(shape) - 1 - dim))
    return gain


def shared_out(key, own, number, rows, number_of, top, most, lean):
    order = jax.random.permutation(key, number_of)
    heavy_load, usual = shares(number_of, rows * top, most, lean, True), shares(number_of, rows * top, most, lean, False)
    places = jnp.arange(number_of)

    def named(tallies, turn):
        used = int((tallies > 0).sum())
        fixed = max(1, used // 4)
        moved = fixed + (places - fixed + turn * (used - fixed)) % max(1, number_of - fixed)
        return jnp.zeros((number_of,), jnp.int32).at[order[jnp.where(places < fixed, places, moved)]].set(jnp.asarray(tallies, jnp.int32))

    tallies = jnp.where(number % 4 == 0, named(heavy_load, number // 4), named(usual, number - number // 4 - 1))
    mixed = jax.random.permutation(jax.random.fold_in(own, 3), number_of)
    giver, taker = mixed[0:number_of // 2 * 2:2], mixed[1:number_of // 2 * 2:2]
    slack = jnp.minimum(tallies[giver] - 1, most - tallies[taker]) // 2
    slack = jnp.where((giver == order[0]) | (taker == order[0]) | (tallies[taker] == 0), 0, jnp.maximum(slack, 0))
    moved = jax.random.randint(jax.random.fold_in(own, 4), (number_of // 2,), 0, 1 << 20) % (slack + 1)
    tallies = tallies.at[giver].add(-moved).at[taker].add(moved)
    members = jnp.searchsorted(jnp.cumsum(tallies), jnp.arange(rows * top), side="right").astype(jnp.int32)
    table = members.reshape(top, rows).T
    table = table[jax.random.permutation(jax.random.fold_in(own, 1), rows)]
    turn = jax.random.randint(jax.random.fold_in(own, 2), (rows, 1), 0, top)
    return jnp.take_along_axis(table, (jnp.arange(top)[None, :] + turn) % top, axis=1)


def shares(amount, total, most, skew, full):
    portions = [(1 << 20) // math.isqrt(grade ** skew) + 1 for grade in range(1, amount + 1)]
    largest = most if full else min(most, max(-(-total // amount), total * portions[0] // sum(portions)))
    least = 1 if total - largest >= amount - 1 else 0
    given, spare = [largest] + [least] * (amount - 1), total - largest - least * (amount - 1)
    while spare > 0:
        movable = [i for i in range(1, amount) if given[i] < largest] or [i for i in range(1, amount) if given[i] < most]
        whole, left = sum([portions[i] for i in movable]), spare
        for i in movable:
            extra = min(most - given[i], max(1, left * portions[i] // whole), spare)
            given[i] = given[i] + extra
            spare = spare - extra
    return np.array(given)


def noise(key, extent, scale, limit, shards=(), kind=jnp.bfloat16):
    level = steps_of(key, extent, shards, -0.22, 0.18) if shards else 1.0
    result = jax.random.normal(key, extent, jnp.float32) * scale * level
    return jnp.minimum(jnp.maximum(result, -limit), limit).astype(kind)


def setup_inputs(seed: int = 0) -> dict:
    arg_keys = jax.random.split(jax.random.key(seed), 9)
    grad_out = noise(arg_keys[0], (TOKENS, D), 1.0, 6.0, ((0, 8), (1, 4)))
    probs = jnp.clip(0.05 + 0.35 * jax.random.uniform(arg_keys[1], (TOKENS, TOPK), jnp.float32) ** steps_of(arg_keys[1], (TOKENS, TOPK), ((0, 8),), -0.2, 0.2), 0.05, 0.4)
    expert_ids_keys = jax.random.split(jax.random.fold_in(arg_keys[2], 1), TOKENS // TOK_DEV)
    expert_ids_turns = jax.random.permutation(jax.random.fold_in(arg_keys[2], 3), TOKENS // TOK_DEV)
    expert_ids = jax.vmap(lambda own, number: shared_out(jax.random.fold_in(arg_keys[2], 2), own, number, TOK_DEV, EXPERTS, TOPK, CAP, 2))(expert_ids_keys, expert_ids_turns).reshape((TOKENS, TOPK))
    w_gate = noise(arg_keys[3], (EXPERTS, FF, D), D ** -0.5, 0.09375, ((0, 8), (1, 4)))
    w_up = noise(arg_keys[4], (EXPERTS, FF, D), D ** -0.5, 0.09375, ((0, 8), (1, 4)))
    w_down = noise(arg_keys[5], (EXPERTS, FF, D), FF ** -0.5, 0.15625, ((0, 8), (1, 4)))
    saved_gate = noise(arg_keys[6], (EXPERTS, FF, SLOTS), 0.5, 3.0, ((0, 8), (1, 4)))
    saved_up = noise(arg_keys[7], (EXPERTS, FF, SLOTS), 0.5, 3.0, ((0, 8), (1, 4)))
    return dict(grad_out=grad_out, probs=probs, expert_ids=expert_ids, w_gate=w_gate, w_up=w_up, w_down=w_down, saved_gate=saved_gate, saved_up=saved_up)


def slot_index(expert_ids):
    blocks = expert_ids.reshape(N_EXPERT, TOK_DEV * TOPK)
    onehot = (blocks[:, :, None] == jnp.arange(EXPERTS, dtype=jnp.int32)[None, None, :]).astype(jnp.int32)
    before = jnp.cumsum(onehot, axis=1) - onehot
    position = jnp.sum(before * onehot, axis=2).astype(jnp.int32)
    source = jnp.arange(N_EXPERT, dtype=jnp.int32)[:, None]
    flat = blocks * SLOTS + source * CAP + position
    return flat.reshape(-1).astype(jnp.int32)


def reference(grad_out, probs, expert_ids, w_gate, w_up, w_down, saved_gate, saved_up):
    flat = slot_index(expert_ids)
    owner = (jnp.arange(TOKENS * TOPK, dtype=jnp.int32) // TOPK).astype(jnp.int32)
    table = jnp.full((EXPERTS * SLOTS,), TOKENS, jnp.int32).at[flat].set(owner)
    padded = jnp.concatenate([grad_out, jnp.zeros((1, D), jnp.bfloat16)], axis=0)
    group = FF // N_SECTION

    def expert_step(item):
        table_row, gate_rows, up_rows, down_rows, gate_saved, up_saved = item
        dispatched = padded[table_row]
        hidden_grad = jnp.dot(dispatched, down_rows.T, preferred_element_type=jnp.float32)
        gate_act = gate_saved.astype(jnp.float32).T
        up_act = up_saved.astype(jnp.float32).T
        sigmoid_gate = jax.nn.sigmoid(gate_act)
        silu_gate = gate_act * sigmoid_gate
        router = jnp.sum(silu_gate * up_act * hidden_grad, axis=1).astype(jnp.bfloat16)
        gate_grad = (hidden_grad * up_act * sigmoid_gate * (1.0 + gate_act * (1.0 - sigmoid_gate))).astype(jnp.bfloat16)
        up_grad = (hidden_grad * silu_gate).astype(jnp.bfloat16)
        gate_parts = gate_grad.astype(jnp.float32).reshape(SLOTS, N_SECTION, group)
        up_parts = up_grad.astype(jnp.float32).reshape(SLOTS, N_SECTION, group)
        gate_mat = gate_rows.astype(jnp.float32).reshape(N_SECTION, group, D)
        up_mat = up_rows.astype(jnp.float32).reshape(N_SECTION, group, D)
        partial_value = jnp.einsum('srf,rfd->rsd', gate_parts, gate_mat) + jnp.einsum('srf,rfd->rsd', up_parts, up_mat)
        rounded = lax.optimization_barrier(partial_value.astype(jnp.bfloat16))
        expert_grad = jnp.sum(rounded.astype(jnp.float32), axis=0).astype(jnp.bfloat16)
        return expert_grad, router

    expert_grad, router_grad = lax.map(expert_step, (table.reshape(EXPERTS, SLOTS), w_gate, w_up, w_down, saved_gate, saved_up))
    picked = expert_grad.reshape(EXPERTS * SLOTS, D)[flat].reshape(TOKENS, TOPK, D)
    grad_in = jnp.sum(picked.astype(jnp.float32) * probs[:, :, None], axis=1).astype(jnp.bfloat16)
    grad_probs = router_grad.reshape(-1)[flat].reshape(TOKENS, TOPK)
    return grad_in, grad_probs
```

```python
import functools

import jax
import jax.numpy as jnp
from jax import lax
from jax.experimental import pallas as pl
from jax.experimental.pallas import tpu as pltpu
from jax.sharding import PartitionSpec as P

CHUNKS = 2
F32, BF16 = jnp.float32, jnp.bfloat16
ROWS_BY_ROWS = (((1,), (1,)), ((), ()))
VMEM = 40 << 20


def coefficient_kernel(slot_ref, prob_ref, gate_ref, up_ref, cg_ref, cu_ref, cr_ref):
    rows, slots = slot_ref.shape[0], gate_ref.shape[2]
    width = gate_ref.shape[1]
    column = lax.broadcasted_iota(jnp.int32, (rows, slots), 1)
    for e in range(gate_ref.shape[0]):
        pick = jnp.where(slot_ref[:, e : e + 1] == column, 1.0, 0.0).astype(BF16)
        g = lax.dot_general(pick, gate_ref[e], ROWS_BY_ROWS, preferred_element_type=F32)
        u = lax.dot_general(pick, up_ref[e], ROWS_BY_ROWS, preferred_element_type=F32)
        p = prob_ref[:, e : e + 1]
        sg = 1.0 / (1.0 + jnp.exp(-g))
        silu = g * sg
        span = slice(e * width, (e + 1) * width)
        cg_ref[:, span] = u * sg * (1.0 + g * (1.0 - sg)) * p
        cu_ref[:, span] = silu * p
        cr_ref[:, span] = silu * u


def coefficients(slot, prob, saved_gate, saved_up, tile):
    total, experts = slot.shape
    width = saved_gate.shape[1]
    row = lambda n: pl.BlockSpec((tile, n), lambda i: (i, 0))
    whole = pl.BlockSpec(saved_gate.shape, lambda i: (0, 0, 0))
    return pl.pallas_call(
        coefficient_kernel,
        grid=(total // tile,),
        in_specs=[row(experts), row(experts), whole, whole],
        out_specs=[row(experts * width)] * 3,
        out_shape=[jax.ShapeDtypeStruct((total, experts * width), F32)] * 3,
        compiler_params=pltpu.CompilerParams(vmem_limit_bytes=VMEM),
        name="coefficients",
    )(slot, prob, saved_gate, saved_up)


def hidden_kernel(order, experts, z_ref, *refs):
    blocks = refs[: len(refs) - 8]
    wd_ref, cg_ref, cu_ref, cr_ref, ag_ref, au_ref, r_ref, acc_ref = refs[len(refs) - 8 :]
    step, last = pl.program_id(0), pl.num_programs(0) - 1
    x = jnp.concatenate([blocks[i][j, 0] for i, j in order], axis=0)
    part = lax.dot_general(x, wd_ref[...], ROWS_BY_ROWS, preferred_element_type=F32)

    @pl.when(step == 0)
    def _():
        acc_ref[...] = part

    @pl.when(step > 0)
    def _():
        acc_ref[...] += part

    @pl.when(step == last)
    def _():
        h = acc_ref[...]
        ag_ref[...] = (h * cg_ref[...]).astype(BF16)
        au_ref[...] = (h * cu_ref[...]).astype(BF16)
        terms = h * cr_ref[...]
        width = terms.shape[1] // experts
        for e in range(experts):
            r_ref[:, e : e + 1] = jnp.sum(
                terms[:, e * width : (e + 1) * width], axis=1, keepdims=True
            )


def hidden(z, blocks, order, w_down, coefs, chunk, experts):
    steps, rows, span = blocks[0].shape[1:]
    total = rows * len(order)
    units = w_down.shape[0]
    block = lambda n: pl.BlockSpec((n, 1, rows, span), lambda s, z: (0, s, 0, 0))
    coef = pl.BlockSpec((total, units), lambda s, z: (chunk, 0))
    full = lambda n: pl.BlockSpec((total, n), lambda s, z: (0, 0))
    return pl.pallas_call(
        functools.partial(hidden_kernel, order, experts),
        grid_spec=pltpu.PrefetchScalarGridSpec(
            num_scalar_prefetch=1,
            grid=(steps,),
            in_specs=[block(b.shape[0]) for b in blocks]
            + [pl.BlockSpec((units, span), lambda s, z: (0, lax.rem(z[0] + s, steps)))]
            + [coef] * 3,
            out_specs=[full(units), full(units), full(experts)],
            scratch_shapes=[pltpu.VMEM((total, units), F32)],
        ),
        out_shape=[jax.ShapeDtypeStruct((total, units), BF16)] * 2
        + [jax.ShapeDtypeStruct((total, experts), F32)],
        compiler_params=pltpu.CompilerParams(vmem_limit_bytes=VMEM),
        name="hidden",
    )(z, *blocks, w_down, *coefs)


def out_kernel(z_ref, ag_ref, au_ref, wg_ref, wu_ref, *outs):
    y = jnp.dot(ag_ref[...], wg_ref[...], preferred_element_type=F32)
    y = y + jnp.dot(au_ref[...], wu_ref[...], preferred_element_type=F32)
    y = y.astype(BF16)
    at = 0
    for out in outs:
        count, _, rows, _ = out.shape
        for j in range(count):
            out[j, 0] = y[at : at + rows]
            at += rows


def expand(z, ag, au, w_gate, w_up, steps, rows, counts):
    total, units = ag.shape
    span = w_gate.shape[1] // steps
    whole = pl.BlockSpec((total, units), lambda s, z: (0, 0))
    weight = pl.BlockSpec((units, span), lambda s, z: (0, lax.rem(z[0] + s, steps)))
    return pl.pallas_call(
        out_kernel,
        grid_spec=pltpu.PrefetchScalarGridSpec(
            num_scalar_prefetch=1,
            grid=(steps,),
            in_specs=[whole, whole, weight, weight],
            out_specs=[
                pl.BlockSpec((n, 1, rows, span), lambda s, z: (0, s, 0, 0)) for n in counts
            ],
        ),
        out_shape=[jax.ShapeDtypeStruct((n, steps, rows, span), BF16) for n in counts],
        compiler_params=pltpu.CompilerParams(vmem_limit_bytes=VMEM),
        name="expand",
    )(z, ag, au, w_gate, w_up)


def add(*terms):
    return functools.reduce(lambda a, b: a + b, [t.astype(F32) for t in terms])


def local(grad_out, probs, expert_ids, w_gate, w_up, w_down, saved_gate, saved_up):
    groups, sections = lax.axis_size("expert"), lax.axis_size("section")
    me, z = lax.axis_index("expert"), lax.axis_index("section")
    experts, units, features = w_gate.shape
    slots = saved_gate.shape[2]
    capacity = slots // groups
    tokens, topk = expert_ids.shape
    span = grad_out.shape[1]
    rows = tokens // CHUNKS
    square = groups == 8

    core = me % 2
    near = jnp.where(core == 0, 2, 4)
    far = 6 - near

    def swap(x, even, odd):
        return lax.ppermute(x, "expert", [(i, i ^ (even, odd)[i % 2]) for i in range(groups)])

    def shift(x, by):
        return lax.ppermute(x, "section", [(i, (i + by) % sections) for i in range(sections)])

    if square:
        owners = jnp.stack([me, me ^ near, me ^ near ^ 1, me ^ 6, me ^ 1, me ^ 1 ^ far, me ^ far, me ^ 7])
        order = ((0, 0), (1, 0), (1, 1), (3, 0), (0, 1), (2, 0), (2, 1), (4, 0))
        counts = (groups // 2, groups // 2)
    else:
        owners = jnp.arange(groups)
        order = tuple((0, i) for i in range(groups))
        counts = (groups,)

    routing = jnp.concatenate([expert_ids.T.astype(F32), probs.T], axis=0)[None]
    if square:
        for bit in (2, 4, 1):
            routing = jnp.concatenate([routing, swap(routing, bit, bit)], axis=0)
        even = routing[jnp.array([0, 1, 5, 3, 4, 6, 2, 7])]
        odd = routing[jnp.array([0, 2, 6, 3, 4, 5, 1, 7])]
        routing = jnp.where(core == 0, even, odd)
    else:
        routing = lax.all_gather(routing, "expert", axis=0, tiled=True)
    mine = (me * experts + jnp.arange(experts)).astype(F32)
    chosen = routing[:, None, :topk] == mine[None, :, None, None]
    weight = jnp.sum(jnp.where(chosen, routing[:, None, topk:], 0.0), axis=2)
    named = jnp.any(chosen, axis=2)
    earlier = jnp.arange(tokens)[:, None] < jnp.arange(tokens)[None, :]
    position = lax.dot_general(
        named.astype(BF16), earlier.astype(BF16), (((2,), (0,)), ((), ())), preferred_element_type=F32
    ).astype(jnp.int32)
    slot = jnp.where(named, owners[:, None, None] * capacity + position, -1)

    def by_chunk(x):
        x = x.reshape(groups, experts, CHUNKS, rows)
        return x.transpose(2, 0, 3, 1).reshape(CHUNKS * groups * rows, experts)

    coefs = coefficients(by_chunk(slot), by_chunk(weight), saved_gate, saved_up, min(512, groups * rows))

    flat = lambda w: w.reshape(experts * units, features)
    start = z.astype(jnp.int32).reshape(1)
    results, routers = [], []
    for c in range(CHUNKS):
        piece = grad_out[c * rows : (c + 1) * rows]
        own = jnp.stack([piece] + [shift(piece, -i) for i in range(1, sections)])
        if square:
            pair = jnp.stack([own, swap(own, 1, 1)])
            first = swap(pair, 2, 4)
            second = swap(first[:1], 4, 2)
            blocks = [pair, first, swap(first, 1, 1), second, swap(second, 1, 1)]
        else:
            blocks = [lax.all_gather(own, "expert")]
        ag, au, router = hidden(start, blocks, order, flat(w_down), coefs, c, experts)
        routers.append(router.reshape(groups, rows, experts))
        outs = expand(start, ag, au, flat(w_gate), flat(w_up), sections, rows, counts)
        if square:
            kept = add(outs[0], swap(outs[1], 1, 1)).astype(BF16)
            diagonal = swap(kept[3], 4, 2)
            sent = jnp.stack([add(kept[1], diagonal).astype(BF16), kept[2]])
            received = swap(sent, 2, 4)
            total = add(kept[0], received[0], swap(received[1], 1, 1))
        else:
            total = lax.psum_scatter(outs[0], "expert", scatter_dimension=0, tiled=True)[0].astype(F32)
        sums = total.astype(BF16)
        results.append(add(total[0], *[shift(sums[i], i) for i in range(1, sections)]).astype(BF16))
    grad_in = jnp.concatenate(results, axis=0)

    router = jnp.concatenate(routers, axis=1)
    if square:
        for bit in range(sections.bit_length() - 1):
            by = 1 << bit
            router = router + lax.ppermute(router, "section", [(i, i ^ by) for i in range(sections)])
        even = router[jnp.array([0, 4, 1, 2, 6, 5, 3, 7])]
        odd = router[jnp.array([0, 4, 6, 5, 1, 2, 3, 7])]
        router = jnp.where(core == 0, even, odd)
        router = router.transpose(0, 2, 1)
        gathered = router[None]
        for bit in (1, 2, 4):
            gathered = jnp.concatenate([gathered, swap(gathered, bit, bit)], axis=0)
        back = jnp.stack([gathered[q, q] for q in range(groups)])
        source = me ^ jnp.arange(groups)
    else:
        router = lax.psum(router, "section").transpose(0, 2, 1)
        back = lax.all_to_all(router, "expert", split_axis=0, concat_axis=0)
        source = jnp.arange(groups)
    number = (source[:, None] * experts + jnp.arange(experts)).reshape(-1)
    back = back.reshape(groups * experts, tokens)
    match = expert_ids[None] == number[:, None, None]
    grad_probs = jnp.sum(jnp.where(match, back[:, :, None], 0.0), axis=0).astype(BF16)
    return (grad_in, grad_probs)


def solution(mesh):
    placed = (
        P("expert", "section"),
        P("expert", None),
        P("expert", None),
        P("expert", "section", None),
        P("expert", "section", None),
        P("expert", "section", None),
        P("expert", "section", None),
        P("expert", "section", None),
    )
    return jax.shard_map(
        local,
        mesh=mesh,
        in_specs=placed,
        out_specs=(P("expert", "section"), P("expert", None)),
        check_vma=False,
    )
```

```python
import functools

import jax
import jax.numpy as jnp
from jax import lax
from jax.experimental import pallas as pl
from jax.experimental.pallas import tpu as pltpu
from jax.sharding import PartitionSpec as P

F32, BF16 = jnp.float32, jnp.bfloat16
ROWS_BY_ROWS = (((1,), (1,)), ((), ()))
VMEM = 48 << 20


def coefficient_kernel(slot_ref, prob_ref, gate_ref, up_ref, cg_ref, cu_ref, cr_ref):
    rows, slots = slot_ref.shape[0], gate_ref.shape[2]
    width = gate_ref.shape[1]
    column = lax.broadcasted_iota(jnp.int32, (rows, slots), 1)
    for e in range(gate_ref.shape[0]):
        pick = jnp.where(slot_ref[:, e : e + 1] == column, 1.0, 0.0).astype(BF16)
        g = lax.dot_general(pick, gate_ref[e], ROWS_BY_ROWS, preferred_element_type=F32)
        u = lax.dot_general(pick, up_ref[e], ROWS_BY_ROWS, preferred_element_type=F32)
        p = prob_ref[:, e : e + 1]
        sg = 1.0 / (1.0 + jnp.exp(-g))
        silu = g * sg
        span = slice(e * width, (e + 1) * width)
        cg_ref[:, span] = u * sg * (1.0 + g * (1.0 - sg)) * p
        cu_ref[:, span] = silu * p
        cr_ref[:, span] = silu * u


def coefficients(slot, prob, saved_gate, saved_up, tile):
    total, experts = slot.shape
    width = saved_gate.shape[1]
    row = lambda n: pl.BlockSpec((tile, n), lambda i: (i, 0))
    whole = pl.BlockSpec(saved_gate.shape, lambda i: (0, 0, 0))
    return pl.pallas_call(
        coefficient_kernel,
        grid=(total // tile,),
        in_specs=[row(experts), row(experts), whole, whole],
        out_specs=[row(experts * width)] * 3,
        out_shape=[jax.ShapeDtypeStruct((total, experts * width), F32)] * 3,
        compiler_params=pltpu.CompilerParams(vmem_limit_bytes=VMEM),
        name="coefficients",
    )(slot, prob, saved_gate, saved_up)


def rows_of(refs, k):
    parts = [r[:, k].reshape(r.shape[0] * r.shape[2], r.shape[3]) for r in refs]
    return parts[0] if len(parts) == 1 else jnp.concatenate(parts, axis=0)


def products(groups, wd_refs):
    total, at = None, 0
    for refs in groups:
        for k in range(refs[0].shape[1]):
            part = lax.dot_general(
                rows_of(refs, k), wd_refs[at][...], ROWS_BY_ROWS, preferred_element_type=F32
            )
            total = part if total is None else total + part
            at += 1
    return total


def split(refs, sizes):
    out, at = [], 0
    for n in sizes:
        out.append(refs[at : at + n])
        at += n
    return out, refs[at:]


def early_kernel(sizes, pieces, z_ref, *refs):
    groups, refs = split(refs, sizes)
    wd_refs, (h_ref,) = refs[:pieces], refs[pieces:]
    h_ref[...] = products(groups, wd_refs)


def late_kernel(sizes, pieces, width, z_ref, *refs):
    groups, refs = split(refs, sizes)
    wd_refs, refs = refs[:pieces], refs[pieces:]
    h_ref, cg_ref, cu_ref, cr_ref, ag_ref, au_ref, r_ref = refs
    h = h_ref[...] + products(groups, wd_refs)
    ag_ref[...] = (h * cg_ref[...]).astype(BF16)
    au_ref[...] = (h * cu_ref[...]).astype(BF16)
    terms = h * cr_ref[...]
    tile = terms.shape[1]
    unit = pl.program_id(0) * tile + lax.broadcasted_iota(jnp.int32, terms.shape, 1)

    @pl.when(pl.program_id(0) == 0)
    def _():
        r_ref[...] = jnp.zeros_like(r_ref)

    for e in range(r_ref.shape[1]):
        own = (unit >= e * width) & (unit < (e + 1) * width)
        r_ref[:, e : e + 1] += jnp.sum(jnp.where(own, terms, 0.0), axis=1, keepdims=True)


def tile_of(n):
    return 256 if n % 256 == 0 else 128 if n % 128 == 0 else n


def hidden_specs(groups, w_down):
    units = w_down.shape[0]
    tile = tile_of(units)
    operands, specs, weights = [], [], []
    for first, blocks in groups:
        span = blocks[0].shape[3]
        for b in blocks:
            operands.append(b)
            specs.append(pl.BlockSpec(b.shape, lambda n, z: (0, 0, 0, 0)))
        for k in range(blocks[0].shape[1]):
            weights.append(pl.BlockSpec((tile, span), lambda n, z, i=first + k: (n, z[0] ^ i)))
    return operands + [w_down] * len(weights), specs + weights, len(weights), tile


def hidden_early(z, groups, w_down):
    operands, specs, pieces, tile = hidden_specs(groups, w_down)
    units = w_down.shape[0]
    total = sum(b.shape[0] * b.shape[2] for b in groups[0][1])
    return pl.pallas_call(
        functools.partial(early_kernel, [len(b) for _, b in groups], pieces),
        grid_spec=pltpu.PrefetchScalarGridSpec(
            num_scalar_prefetch=1,
            grid=(units // tile,),
            in_specs=specs,
            out_specs=pl.BlockSpec((total, tile), lambda n, z: (0, n)),
        ),
        out_shape=jax.ShapeDtypeStruct((total, units), F32),
        compiler_params=pltpu.CompilerParams(vmem_limit_bytes=VMEM),
        name="hidden_early",
    )(z, *operands)


def hidden_late(z, groups, w_down, early, coefs, experts):
    operands, specs, pieces, tile = hidden_specs(groups, w_down)
    total, units = early.shape
    column = pl.BlockSpec((total, tile), lambda n, z: (0, n))
    return pl.pallas_call(
        functools.partial(late_kernel, [len(b) for _, b in groups], pieces, units // experts),
        grid_spec=pltpu.PrefetchScalarGridSpec(
            num_scalar_prefetch=1,
            grid=(units // tile,),
            in_specs=specs + [column] * 4,
            out_specs=[column, column, pl.BlockSpec((total, experts), lambda n, z: (0, 0))],
        ),
        out_shape=[jax.ShapeDtypeStruct((total, units), BF16)] * 2
        + [jax.ShapeDtypeStruct((total, experts), F32)],
        compiler_params=pltpu.CompilerParams(vmem_limit_bytes=VMEM),
        name="hidden_late",
    )(z, *operands, early, *coefs)


def expand_kernel(places, z_ref, ag_ref, au_ref, wg_ref, wu_ref, *outs):
    rows, width = outs[0].shape[2:]
    tile = tile_of(width)
    for at in range(0, width, tile):
        span = slice(at, at + tile)
        y = jnp.dot(ag_ref[...], wg_ref[:, span], preferred_element_type=F32)
        y = (y + jnp.dot(au_ref[...], wu_ref[:, span], preferred_element_type=F32)).astype(BF16)
        for i, (out, j) in enumerate(places):
            outs[out][j, 0, :, span] = y[i * rows : (i + 1) * rows]


def expand(z, first, pieces, ag, au, w_gate, w_up, sections, rows, places):
    total, units = ag.shape
    span = w_gate.shape[1] // sections
    half = max(span // 2, 128)
    per = span // half
    counts = [sum(1 for o, _ in places if o == n) for n in range(1 + max(o for o, _ in places))]
    whole = pl.BlockSpec((total, units), lambda k, j, z: (0, 0))
    weight = pl.BlockSpec((units, half), lambda k, j, z: (0, (z[0] ^ (first + k)) * per + j))
    return pl.pallas_call(
        functools.partial(expand_kernel, places),
        grid_spec=pltpu.PrefetchScalarGridSpec(
            num_scalar_prefetch=1,
            grid=(pieces, per),
            in_specs=[whole, whole, weight, weight],
            out_specs=[pl.BlockSpec((n, 1, rows, half), lambda k, j, z: (0, k, 0, j)) for n in counts],
        ),
        out_shape=[jax.ShapeDtypeStruct((n, pieces, rows, span), BF16) for n in counts],
        compiler_params=pltpu.CompilerParams(vmem_limit_bytes=VMEM),
        name="expand",
    )(z, ag, au, w_gate, w_up)


def add(*terms):
    return functools.reduce(lambda a, b: a + b, [t.astype(F32) for t in terms])


def after(x, *others):
    return lax.optimization_barrier((x, *others))[0]


def local(grad_out, probs, expert_ids, w_gate, w_up, w_down, saved_gate, saved_up):
    groups, sections = lax.axis_size("expert"), lax.axis_size("section")
    me, z = lax.axis_index("expert"), lax.axis_index("section")
    experts, units, features = w_gate.shape
    slots = saved_gate.shape[2]
    capacity = slots // groups
    tokens, topk = expert_ids.shape
    square = groups == 8

    core = me % 2
    near = jnp.where(core == 0, 2, 4)
    far = 6 - near

    def swap(x, even, odd):
        return lax.ppermute(x, "expert", [(i, i ^ (even, odd)[i % 2]) for i in range(groups)])

    def across(x, by):
        return lax.ppermute(x, "section", [(i, i ^ by) for i in range(sections)])

    if square:
        owners = jnp.stack([me, me ^ 1, me ^ near, me ^ near ^ 1, me ^ 1 ^ far, me ^ far, me ^ 6, me ^ 7])
        places = ((0, 0), (1, 0), (0, 1), (0, 2), (1, 1), (1, 2), (0, 3), (1, 3))
    else:
        owners = jnp.arange(groups)
        places = tuple((0, i) for i in range(groups))

    def gather(own):
        if not square:
            return [lax.all_gather(own, "expert", axis=0, tiled=True)]
        pair = jnp.concatenate([own, swap(own, 1, 1)])
        first = swap(pair, 2, 4)
        second = swap(first[:1], 4, 2)
        return [pair, first, swap(first, 1, 1), second, swap(second, 1, 1)]

    start = z.astype(jnp.int32).reshape(1)
    piece = grad_out[None]
    received = [piece] + [across(piece, i) for i in (1, 2) if i < sections]
    for i in range(3, sections):
        received.append(across(after(piece, received[i - 2]), i))
    lots = ((0, 1), (1, 3), (3, sections))
    lots = [(a, gather(jnp.stack(received[a:b], axis=1))) for a, b in lots if a < b]

    routing = jnp.concatenate([expert_ids.T.astype(F32), probs.T], axis=0)[None]
    if square:
        for bit in (2, 4, 1):
            routing = jnp.concatenate([routing, swap(routing, bit, bit)], axis=0)
        even = routing[jnp.array([0, 4, 1, 5, 6, 2, 3, 7])]
        odd = routing[jnp.array([0, 4, 2, 6, 5, 1, 3, 7])]
        routing = jnp.where(core == 0, even, odd)
    else:
        routing = lax.all_gather(routing, "expert", axis=0, tiled=True)
    mine = (me * experts + jnp.arange(experts)).astype(F32)
    chosen = routing[:, None, :topk] == mine[None, :, None, None]
    weight = jnp.sum(jnp.where(chosen, routing[:, None, topk:], 0.0), axis=2)
    named = jnp.any(chosen, axis=2)
    earlier = jnp.arange(tokens)[:, None] < jnp.arange(tokens)[None, :]
    position = lax.dot_general(
        named.astype(BF16), earlier.astype(BF16), (((2,), (0,)), ((), ())), preferred_element_type=F32
    ).astype(jnp.int32)
    slot = jnp.where(named, owners[:, None, None] * capacity + position, -1)
    by_token = lambda x: x.transpose(0, 2, 1).reshape(groups * tokens, experts)
    coefs = coefficients(by_token(slot), by_token(weight), saved_gate, saved_up, min(512, groups * tokens))

    flat = lambda w: w.reshape(experts * units, features)
    early = hidden_early(start, lots[:2], flat(w_down))
    ag, au, router = hidden_late(start, lots[2:], flat(w_down), early, coefs, experts)

    def reduce(outs):
        if not square:
            return lax.psum_scatter(outs[0], "expert", scatter_dimension=0, tiled=True)[0]
        kept = add(outs[0], swap(outs[1], 1, 1)).astype(BF16)
        diagonal = swap(kept[3], 4, 2)
        sent = jnp.stack([add(kept[1], diagonal).astype(BF16), kept[2]])
        received = swap(sent, 2, 4)
        return add(kept[0], received[0], swap(received[1], 1, 1)).astype(BF16)

    parts = []
    for a, b in ((3, sections), (1, 3), (0, 1)):
        outs = expand(start, a, b - a, ag, au, flat(w_gate), flat(w_up), sections, tokens, places)
        sums = reduce(outs)
        parts += [sums[i - a] if i == 0 else across(sums[i - a], i) for i in range(a, b)]
    grad_in = add(*parts).astype(BF16)

    router = router.reshape(groups, tokens, experts)
    if square:
        for bit in range(sections.bit_length() - 1):
            router = router + across(router, 1 << bit)
        even = router[jnp.array([0, 1, 2, 3, 5, 4, 6, 7])]
        odd = router[jnp.array([0, 1, 5, 4, 2, 3, 6, 7])]
        router = jnp.where(core == 0, even, odd)
        router = router.transpose(0, 2, 1)
        gathered = router[None]
        for bit in (1, 2, 4):
            gathered = jnp.concatenate([gathered, swap(gathered, bit, bit)], axis=0)
        back = jnp.stack([gathered[q, q] for q in range(groups)])
        source = me ^ jnp.arange(groups)
    else:
        router = lax.psum(router, "section").transpose(0, 2, 1)
        back = lax.all_to_all(router, "expert", split_axis=0, concat_axis=0)
        source = jnp.arange(groups)
    number = (source[:, None] * experts + jnp.arange(experts)).reshape(-1)
    back = back.reshape(groups * experts, tokens)
    match = expert_ids[None] == number[:, None, None]
    grad_probs = jnp.sum(jnp.where(match, back[:, :, None], 0.0), axis=0).astype(BF16)
    return (grad_in, grad_probs)


def solution(mesh):
    placed = (
        P("expert", "section"),
        P("expert", None),
        P("expert", None),
        P("expert", "section", None),
        P("expert", "section", None),
        P("expert", "section", None),
        P("expert", "section", None),
        P("expert", "section", None),
    )
    return jax.shard_map(
        local,
        mesh=mesh,
        in_specs=placed,
        out_specs=(P("expert", "section"), P("expert", None)),
        check_vma=False,
    )
```

```python
import functools

import jax
import jax.numpy as jnp
from jax import lax
from jax.experimental import pallas as pl
from jax.experimental.pallas import tpu as pltpu
from jax.sharding import PartitionSpec as P

F32, BF16 = jnp.float32, jnp.bfloat16
ROWS_BY_ROWS = (((1,), (1,)), ((), ()))
VMEM = 48 << 20


def call(kernel, name, grid, in_specs, out_specs, out_shape, operands):
    return pl.pallas_call(
        kernel,
        grid_spec=pltpu.PrefetchScalarGridSpec(
            num_scalar_prefetch=1, grid=grid, in_specs=in_specs, out_specs=out_specs
        ),
        out_shape=out_shape,
        compiler_params=pltpu.CompilerParams(vmem_limit_bytes=VMEM),
        name=name,
    )(*operands)


def coefficient_kernel(capacity, topk, at_ref, info_ref, gate_ref, up_ref, cg_ref, cu_ref, cr_ref):
    blocks, _, tokens = info_ref.shape
    experts, width, slots = gate_ref.shape
    before = lax.broadcasted_iota(jnp.int32, (tokens, tokens), 0)
    earlier = (before < lax.broadcasted_iota(jnp.int32, (tokens, tokens), 1)).astype(BF16)
    columns = []
    for b in range(blocks):
        info = info_ref[b].astype(F32)
        ids, prob = info[:topk], info[topk : 2 * topk] + info[2 * topk : 3 * topk]
        named, weight = [], []
        for e in range(experts):
            chosen = ids == (at_ref[0] + e).astype(F32)
            named.append(jnp.max(jnp.where(chosen, 1.0, 0.0), axis=0, keepdims=True))
            weight.append(jnp.sum(jnp.where(chosen, prob, 0.0), axis=0, keepdims=True))
        named = jnp.concatenate(named, axis=0)
        position = jnp.dot(named.astype(BF16), earlier, preferred_element_type=F32)
        block = at_ref[1 + pl.program_id(0) * blocks + b]
        slot = jnp.where(named > 0.0, position + (block * capacity).astype(F32), -1.0)
        fill = jnp.zeros((8 - 2 * experts, tokens), F32)
        columns.append(jnp.transpose(jnp.concatenate([slot, *weight, fill], axis=0)))
    columns = jnp.concatenate(columns, axis=0)
    number = lax.broadcasted_iota(jnp.int32, (blocks * tokens, slots), 1).astype(F32)
    for e in range(experts):
        pick = jnp.where(columns[:, e : e + 1] == number, 1.0, 0.0).astype(BF16)
        g = lax.dot_general(pick, gate_ref[e], ROWS_BY_ROWS, preferred_element_type=F32)
        u = lax.dot_general(pick, up_ref[e], ROWS_BY_ROWS, preferred_element_type=F32)
        p = columns[:, experts + e : experts + e + 1]
        sg = 1.0 / (1.0 + jnp.exp(-g))
        silu = g * sg
        span = slice(e * width, (e + 1) * width)
        cg_ref[:, span] = (u * sg * (1.0 + g * (1.0 - sg)) * p).astype(BF16)
        cu_ref[:, span] = (silu * p).astype(BF16)
        cr_ref[:, span] = (silu * u).astype(BF16)


def coefficients(at, info, topk, saved_gate, saved_up, capacity):
    blocks, lines, tokens = info.shape
    experts, width, _ = saved_gate.shape
    per = 2 if blocks % 2 == 0 else 1
    whole = pl.BlockSpec(saved_gate.shape, lambda i, at: (0, 0, 0))
    out = pl.BlockSpec((per * tokens, experts * width), lambda i, at: (i, 0))
    return call(
        functools.partial(coefficient_kernel, capacity, topk),
        "coefficients",
        (blocks // per,),
        [pl.BlockSpec((per, lines, tokens), lambda i, at: (i, 0, 0)), whole, whole],
        [out] * 3,
        [jax.ShapeDtypeStruct((blocks * tokens, experts * width), BF16)] * 3,
        (at, info, saved_gate, saved_up),
    )


def products(refs, wd_refs):
    total = None
    for k, wd_ref in enumerate(wd_refs):
        parts = [r[:, k].reshape(r.shape[0] * r.shape[2], r.shape[3]) for r in refs]
        x = parts[0] if len(parts) == 1 else jnp.concatenate(parts, axis=0)
        part = lax.dot_general(x, wd_ref[...], ROWS_BY_ROWS, preferred_element_type=F32)
        total = part if total is None else total + part
    return total


def early_kernel(blocks, pieces, z_ref, *refs):
    rows, wd_refs, rest = refs[:blocks], refs[blocks : blocks + pieces], refs[blocks + pieces :]
    h = products(rows, wd_refs)
    rest[-1][...] = h if len(rest) == 1 else rest[0][...] + h


def late_kernel(blocks, pieces, width, moves, z_ref, *refs):
    rows, wd_refs, rest = refs[:blocks], refs[blocks : blocks + pieces], refs[blocks + pieces :]
    h_ref, cg_ref, cu_ref, cr_ref, ag_ref, au_ref, r_ref = rest
    h = h_ref[...] + products(rows, wd_refs)
    ag = (h * cg_ref[...].astype(F32)).astype(BF16)
    au = (h * cu_ref[...].astype(F32)).astype(BF16)
    tokens = h.shape[0] // len(moves)
    for i, j in enumerate(moves):
        to, of = slice(j * tokens, (j + 1) * tokens), slice(i * tokens, (i + 1) * tokens)
        ag_ref[to], au_ref[to] = ag[of], au[of]
    terms = h * cr_ref[...].astype(F32)
    unit = pl.program_id(0) * terms.shape[1] + lax.broadcasted_iota(jnp.int32, terms.shape, 1)

    @pl.when(pl.program_id(0) == 0)
    def _():
        r_ref[...] = jnp.zeros_like(r_ref)

    for e in range(r_ref.shape[1]):
        own = (unit >= e * width) & (unit < (e + 1) * width)
        r_ref[:, e : e + 1] += jnp.sum(jnp.where(own, terms, 0.0), axis=1, keepdims=True)


def tile_of(n):
    return 256 if n % 256 == 0 else 128 if n % 128 == 0 else n


def hidden(z, first, blocks, tokens, w_down, before=None, coefs=None, experts=None, moves=None):
    units = w_down.shape[0]
    tile = tile_of(units)
    pieces, span = blocks[0].shape[1], blocks[0].shape[3]
    total = tokens * sum(b.shape[0] for b in blocks)
    specs = [pl.BlockSpec((b.shape[0], pieces, tokens, span), lambda n, z: (0, 0, 0, 0)) for b in blocks]
    specs += [pl.BlockSpec((tile, span), lambda n, z, i=first + k: (n, z[0] ^ i)) for k in range(pieces)]
    operands = [z, *blocks] + [w_down] * pieces
    column = pl.BlockSpec((total, tile), lambda n, z: (0, n))
    if before is not None:
        specs, operands = specs + [column], operands + [before]
    grid = (units // tile,)
    if coefs is None:
        out = jax.ShapeDtypeStruct((total, units), F32)
        kernel = functools.partial(early_kernel, len(blocks), pieces)
        return call(kernel, "hidden_early", grid, specs, column, out, operands)
    kernel = functools.partial(late_kernel, len(blocks), pieces, units // experts, moves)
    outs = [column, column, pl.BlockSpec((total, experts), lambda n, z: (0, 0))]
    shapes = [jax.ShapeDtypeStruct((total, units), BF16)] * 2 + [jax.ShapeDtypeStruct((total, experts), F32)]
    return call(kernel, "hidden_late", grid, specs + [column] * 3, outs, shapes, [*operands, *coefs])


def expand_kernel(counts, adds, z_ref, ag_ref, au_ref, wg_ref, wu_ref, *refs):
    more, outs = refs[: int(adds)], refs[int(adds) :]
    rows, width = outs[0].shape[2:]
    tile = tile_of(width)
    for at in range(0, width, tile):
        span = slice(at, at + tile)
        y = jnp.dot(ag_ref[...], wg_ref[:, span], preferred_element_type=F32)
        y = y + jnp.dot(au_ref[...], wu_ref[:, span], preferred_element_type=F32)
        i = 0
        for out, count in zip(outs, counts):
            for j in range(count):
                part = y[i * rows : (i + 1) * rows]
                if adds:
                    part = part + more[0][i, 0, :, span].astype(F32)
                out[j, 0, :, span] = part.astype(BF16)
                i += 1


def expand(z, first, pieces, part, ag, au, w_gate, w_up, sections, rows, counts, more=None):
    units = ag.shape[1]
    number = sum(counts)
    span = w_gate.shape[1] // sections
    half = max(span // 2, 128)
    per = span // half
    some = pl.BlockSpec((number * rows, units), lambda k, j, z: (part, 0))
    weight = pl.BlockSpec((units, half), lambda k, j, z: (0, (z[0] ^ (first + k)) * per + j))
    block = lambda n: pl.BlockSpec((n, 1, rows, half), lambda k, j, z: (0, k, 0, j))
    extra = [] if more is None else [more]
    return call(
        functools.partial(expand_kernel, counts, more is not None),
        "expand",
        (pieces, per),
        [some, some, weight, weight] + [block(number)] * len(extra),
        [block(n) for n in counts],
        [jax.ShapeDtypeStruct((n, pieces, rows, span), BF16) for n in counts],
        [z, ag, au, w_gate, w_up, *extra],
    )


def add(*terms):
    return functools.reduce(lambda a, b: a + b, [t.astype(F32) for t in terms]).astype(BF16)


def after(x, *others):
    return lax.optimization_barrier((x, *others))[0]


def local(grad_out, probs, expert_ids, w_gate, w_up, w_down, saved_gate, saved_up):
    groups, sections = lax.axis_size("expert"), lax.axis_size("section")
    me, z = lax.axis_index("expert"), lax.axis_index("section")
    experts, units, features = w_gate.shape
    slots = saved_gate.shape[2]
    tokens, topk = expert_ids.shape
    span = grad_out.shape[1]
    square = groups == 8
    flat = lambda w: w.reshape(experts * units, features)
    w_gate, w_up, w_down = flat(w_gate), flat(w_up), flat(w_down)
    start = z.astype(jnp.int32).reshape(1)

    core = me % 2
    near = jnp.where(core == 0, 2, 4)
    far = 6 - near

    def swap(x, even, odd):
        return lax.ppermute(x, "expert", [(i, i ^ (even, odd)[i % 2]) for i in range(groups)])

    def across(x, by):
        return lax.ppermute(x, "section", [(i, i ^ by) for i in range(sections)])

    if square:
        owners = jnp.stack([me, me ^ 1, me ^ near, me ^ near ^ 1, me ^ 1 ^ far, me ^ far, me ^ 6, me ^ 7])
        moves = (0, 4, 1, 2, 5, 6, 3, 7)
    else:
        owners, moves = jnp.arange(groups), tuple(range(groups))

    high = lax.reduce_precision(probs, 8, 7)
    routing = jnp.concatenate([expert_ids.T.astype(F32), high.T, (probs - high).T], axis=0)
    lines = 3 * topk
    more = -(-lines * tokens // (16 * span)) * 16
    routing = jnp.pad(routing.reshape(-1), (0, more * span - lines * tokens)).reshape(more, span)
    own = jnp.concatenate([grad_out, routing.astype(BF16)], axis=0)[None, None]
    received = [None] + [across(grad_out[None], i) for i in (1, 2) if i < sections]
    if square:
        pair0 = jnp.concatenate([own, swap(own, 1, 1)])
        first0 = swap(pair0, 2, 4)
        second0 = swap(first0[:1], 4, 2)
        lot0 = [pair0, first0, swap(first0, 1, 1), second0, swap(second0, 1, 1)]
    else:
        first0 = lax.all_gather(own, "expert", axis=0, tiled=True)
        lot0 = [first0]
    for i in range(3, sections):
        received.append(across(after(grad_out[None], received[i - 2]), i))

    info = jnp.concatenate([b[:, 0, tokens:] for b in lot0], axis=0).reshape(groups, more * span)
    info = info[:, : lines * tokens].reshape(groups, lines, tokens)
    at = jnp.concatenate([(me * experts)[None], owners]).astype(jnp.int32)

    if square:
        own1 = after(jnp.stack(received[1:3], axis=1), first0)
        pair1 = jnp.concatenate([own1, swap(own1, 1, 1)])
        first1 = swap(after(pair1, second0), 2, 4)
        coefs = coefficients(at, info, topk, saved_gate, saved_up, slots // groups)
        h = hidden(start, 0, lot0, tokens, after(w_down, coefs[0]))
        own2 = jnp.stack(received[3:], axis=1)
        pair2 = jnp.concatenate([own2, swap(own2, 1, 1)])
        first1 = after(first1, h)
        second1 = swap(first1[:1], 4, 2)
        first2 = swap(after(pair2, first1), 2, 4)
        lot1 = [pair1, first1, swap(first1, 1, 1), second1, swap(second1, 1, 1)]
        h = hidden(start, 1, lot1, tokens, after(w_down, first2), h)
        second2 = swap(first2[:1], 4, 2)
        lot2 = [pair2, first2, swap(first2, 1, 1), second2, swap(second2, 1, 1)]
    else:
        coefs = coefficients(at, info, topk, saved_gate, saved_up, slots // groups)
        gather = lambda xs: [lax.all_gather(jnp.stack(xs, axis=1), "expert", axis=0, tiled=True)]
        h = hidden(start, 0, lot0, tokens, w_down)
        h = hidden(start, 1, gather(received[1:3]), tokens, w_down, h)
        lot2 = gather(received[3:])
    ag, au, router = hidden(start, 3, lot2, tokens, w_down, h, coefs, experts, moves)

    lots = ((3, sections), (1, 3), (0, 1))
    weights = (w_gate, w_up)
    half = groups // 2
    last = [router]
    theirs, kept, sent, parts = {}, {}, {}, {}

    def run_expand(n, part, counts, more=None):
        a, b = lots[n]
        outs = expand(start, a, b - a, part, after(ag, *last), au, *weights, sections, tokens, counts, more)
        last[0] = outs[0]
        return outs

    def theirs_step(n):
        theirs[n] = swap(run_expand(n, 1, (half,))[0], 1, 1)

    def mine_step(n):
        alone, two, one = run_expand(n, 0, (1, 2, 1), theirs[n])
        kept[n] = alone, two, swap(one, 4, 2)

    def sent_step(n):
        _, two, one = kept[n]
        two = after(two, *last)
        two = jnp.concatenate([add(two[:1], one), two[1:]])
        last[0] = two
        sent[n] = swap(two, 2, 4)

    def final_step(n):
        a, b = lots[n]
        mine = after(sent[n], *last)
        other = swap(mine[1:], 1, 1)
        sums = [add(kept[n][0][0, k], mine[0, k], other[0, k]) for k in range(b - a)]
        last[0] = sums[0]
        for k, x in enumerate(sums):
            parts[a + k] = x if a + k == 0 else across(x, a + k)

    if square:
        for step, n in (
            (theirs_step, 0),
            (theirs_step, 1),
            (mine_step, 0),
            (mine_step, 1),
            (theirs_step, 2),
            (sent_step, 0),
            (mine_step, 2),
            (sent_step, 1),
            (final_step, 0),
            (sent_step, 2),
            (final_step, 1),
            (final_step, 2),
        ):
            step(n)
    else:
        for n, (a, b) in enumerate(lots):
            sums = lax.psum_scatter(run_expand(n, 0, (groups,))[0], "expert", scatter_dimension=0, tiled=True)[0]
            for k in range(b - a):
                parts[a + k] = sums[k] if a + k == 0 else across(sums[k], a + k)
    grad_in = add(*parts.values())

    router = router.reshape(groups, tokens, experts)
    if square:
        router = after(router, kept[2][0])
        for bit in range(sections.bit_length() - 1):
            router = router + across(router, 1 << bit)
        even = router[jnp.array([0, 1, 2, 3, 5, 4, 6, 7])]
        odd = router[jnp.array([0, 1, 5, 4, 2, 3, 6, 7])]
        router = jnp.where(core == 0, even, odd)
        router = router.transpose(0, 2, 1)
        gathered = router[None]
        for bit in (1, 2, 4):
            gathered = jnp.concatenate([gathered, swap(gathered, bit, bit)], axis=0)
        back = jnp.stack([gathered[q, q] for q in range(groups)])
        source = me ^ jnp.arange(groups)
    else:
        router = lax.psum(router, "section").transpose(0, 2, 1)
        back = lax.all_to_all(router, "expert", split_axis=0, concat_axis=0)
        source = jnp.arange(groups)
    number = (source[:, None] * experts + jnp.arange(experts)).reshape(-1)
    back = back.reshape(groups * experts, tokens)
    match = expert_ids[None] == number[:, None, None]
    grad_probs = jnp.sum(jnp.where(match, back[:, :, None], 0.0), axis=0).astype(BF16)
    return (grad_in, grad_probs)


def solution(mesh):
    placed = (
        P("expert", "section"),
        P("expert", None),
        P("expert", None),
        P("expert", "section", None),
        P("expert", "section", None),
        P("expert", "section", None),
        P("expert", "section", None),
        P("expert", "section", None),
    )
    return jax.shard_map(
        local,
        mesh=mesh,
        in_specs=placed,
        out_specs=(P("expert", "section"), P("expert", None)),
        check_vma=False,
    )
```

```python
import functools

import jax
import jax.numpy as jnp
from jax import lax
from jax.experimental import pallas as pl
from jax.experimental.pallas import tpu as pltpu
from jax.sharding import PartitionSpec as P

F32, BF16 = jnp.float32, jnp.bfloat16
ROWS_BY_ROWS = (((1,), (1,)), ((), ()))
BASE = 10 << 20
WEIGHT = 40


def call(kernel, name, grid, in_specs, out_specs, out_shape, operands, flops, limit, scratch=()):
    outs = out_shape if isinstance(out_shape, list) else [out_shape]
    moved = sum(x.size * x.dtype.itemsize for x in [*operands, *outs])
    return pl.pallas_call(
        kernel,
        grid_spec=pltpu.PrefetchScalarGridSpec(
            num_scalar_prefetch=1,
            grid=grid,
            in_specs=in_specs,
            out_specs=out_specs,
            scratch_shapes=scratch,
        ),
        out_shape=out_shape,
        compiler_params=pltpu.CompilerParams(vmem_limit_bytes=min(limit, 56 << 20)),
        cost_estimate=pl.CostEstimate(flops=WEIGHT * flops, bytes_accessed=moved, transcendentals=0),
        name=name,
    )(*operands)


def coefficient_kernel(capacity, topk, tokens, count, at_ref, *refs):
    lots, (gate_ref, up_ref, cg_ref, cu_ref, cr_ref, columns_ref) = refs[:count], refs[count:]
    experts, width, slots = gate_ref.shape
    span = lots[0].shape[3]

    @pl.when(pl.program_id(0) == 0)
    def _():
        before = lax.broadcasted_iota(jnp.int32, (tokens, tokens), 0)
        earlier = (before < lax.broadcasted_iota(jnp.int32, (tokens, tokens), 1)).astype(BF16)
        infos = [ref[j, 0].astype(F32) for ref in lots for j in range(ref.shape[0])]
        for b, info in enumerate(infos):

            def line(n):
                row, at = divmod(n * tokens, span)
                return info[row : row + 1, at : at + tokens]

            lines = lambda n: jnp.concatenate([line(n * topk + k) for k in range(topk)], axis=0)
            ids, prob = lines(0), lines(1) + lines(2)
            named, weight = [], []
            for e in range(experts):
                chosen = ids == (at_ref[1] + e).astype(F32)
                named.append(jnp.max(jnp.where(chosen, 1.0, 0.0), axis=0, keepdims=True))
                weight.append(jnp.sum(jnp.where(chosen, prob, 0.0), axis=0, keepdims=True))
            named = jnp.concatenate(named, axis=0)
            position = jnp.dot(named.astype(BF16), earlier, preferred_element_type=F32)
            slot = jnp.where(named > 0.0, position + (at_ref[2 + b] * capacity).astype(F32), -1.0)
            fill = jnp.zeros((8 - 2 * experts, tokens), F32)
            columns_ref[b * tokens : (b + 1) * tokens] = jnp.transpose(
                jnp.concatenate([slot, *weight, fill], axis=0)
            )

    rows = cg_ref.shape[0]
    columns = columns_ref[pl.ds(pl.multiple_of(pl.program_id(0) * rows, rows), rows)]
    number = lax.broadcasted_iota(jnp.int32, (rows, slots), 1).astype(F32)
    for e in range(experts):
        pick = jnp.where(columns[:, e : e + 1] == number, 1.0, 0.0).astype(BF16)
        g = lax.dot_general(pick, gate_ref[e], ROWS_BY_ROWS, preferred_element_type=F32)
        u = lax.dot_general(pick, up_ref[e], ROWS_BY_ROWS, preferred_element_type=F32)
        p = columns[:, experts + e : experts + e + 1]
        sg = 1.0 / (1.0 + jnp.exp(-g))
        silu = g * sg
        span = slice(e * width, (e + 1) * width)
        cg_ref[:, span] = (u * sg * (1.0 + g * (1.0 - sg)) * p).astype(BF16)
        cu_ref[:, span] = (silu * p).astype(BF16)
        cr_ref[:, span] = (silu * u).astype(BF16)


def coefficients(at, lots, tokens, topk, saved_gate, saved_up, capacity):
    experts, width, slots = saved_gate.shape
    blocks = sum(x.shape[0] for x in lots)
    tile = (4 if blocks % 4 == 0 else 1) * tokens
    total = blocks * tokens
    more = lots[0].shape[2] - tokens
    whole = pl.BlockSpec(saved_gate.shape, lambda i, at: (0, 0, 0))
    info = lambda x: pl.BlockSpec((x.shape[0], 1, more, x.shape[3]), lambda i, at: (0, 0, tokens // more, 0))
    out = pl.BlockSpec((tile, experts * width), lambda i, at: (i, 0))
    return call(
        functools.partial(coefficient_kernel, capacity, topk, tokens, len(lots)),
        "coefficients",
        (total // tile,),
        [*[info(x) for x in lots], whole, whole],
        [out] * 3,
        [jax.ShapeDtypeStruct((total, experts * width), BF16)] * 3,
        (at, *lots, saved_gate, saved_up),
        4 * total * slots * experts * width,
        2 * BASE,
        [pltpu.VMEM((total, 8), F32)],
    )


def products(plan, refs):
    sums = []
    for before, lots in plan:
        total = None if before is None else refs[before][...]
        for blocks, weights in lots:
            for k, weight in enumerate(weights):
                xs = [refs[i][:, k] for i in blocks]
                xs = [x.reshape(x.shape[0] * x.shape[1], x.shape[2]) for x in xs]
                x = xs[0] if len(xs) == 1 else jnp.concatenate(xs, axis=0)
                y = lax.dot_general(x, refs[weight][...], ROWS_BY_ROWS, preferred_element_type=F32)
                total = y if total is None else total + y
        sums.append(total)
    return sums


def early_kernel(plan, at_ref, *refs):
    for out_ref, h in zip(refs[len(refs) - len(plan) :], products(plan, refs)):
        out_ref[...] = h


def late_kernel(plan, experts, width, moves, at_ref, *refs):
    cg_ref, cu_ref, cr_ref, ag_ref, au_ref, info_ref, r_ref = refs[len(refs) - 7 :]
    total, tile = ag_ref.shape
    tokens = total // len(moves)

    @pl.when(pl.program_id(0) == 0)
    def _():
        r_ref[...] = jnp.zeros_like(r_ref)

    at = 0
    for h in products(plan, refs):
        rows = slice(at, at + h.shape[0])
        ag = (h * cg_ref[rows].astype(F32)).astype(BF16)
        au = (h * cu_ref[rows].astype(F32)).astype(BF16)
        terms = h * cr_ref[rows].astype(F32)
        for i in range(h.shape[0] // tokens):
            j = moves[at // tokens + i]
            to, of = slice(j * tokens, (j + 1) * tokens), slice(i * tokens, (i + 1) * tokens)
            ag_ref[to], au_ref[to] = ag[of], au[of]
        unit = pl.program_id(0) * tile + lax.broadcasted_iota(jnp.int32, terms.shape, 1)
        for e in range(experts):
            own = (unit >= e * width) & (unit < (e + 1) * width)
            r_ref[rows, e : e + 1] += jnp.sum(jnp.where(own, terms, 0.0), axis=1, keepdims=True)
        at += h.shape[0]

    @pl.when(pl.program_id(0) == pl.num_programs(0) - 1)
    def _():
        more, span = info_ref.shape[1:]
        per, count = span // tokens, experts * len(moves)
        for i, j in enumerate(moves):
            value = jnp.transpose(r_ref[i * tokens : (i + 1) * tokens])
            high = value.astype(BF16).astype(F32)
            parts = []
            for x in (high, value - high):
                for n in range(count):
                    own = [jnp.where(at_ref[1] + e == n, x[e : e + 1], 0.0) for e in range(experts)]
                    parts.append(functools.reduce(lambda p, q: p + q, own))
            parts += [jnp.zeros((1, tokens), F32)] * (more * per - len(parts))
            lines = [jnp.concatenate(parts[n : n + per], axis=1) for n in range(0, more * per, per)]
            info_ref[j] = jnp.concatenate(lines, axis=0).astype(BF16)


def tile_of(n):
    return 256 if n % 256 == 0 else 128 if n % 128 == 0 else n


def hidden(at, parts, tokens, w_down, coefs=None, experts=None, moves=None, more=None):
    units = w_down.shape[0]
    tile = tile_of(units)
    specs, operands, weights, plan, sizes, work, held = [], [], {}, [], [], 0, 0

    def operand(x, spec):
        operands.append(x)
        specs.append(spec)
        return len(operands) - 1

    for before, lots in parts:
        size = tokens * sum(b.shape[0] for b in lots[0][1])
        of = None
        if before is not None:
            of = operand(before, pl.BlockSpec((size, tile), lambda n, at: (0, n)))
        steps = []
        for first, blocks in lots:
            pieces, span = blocks[0].shape[1], blocks[0].shape[3]
            whole = lambda b: pl.BlockSpec((b.shape[0], pieces, tokens, span), lambda n, at: (0, 0, 0, 0))
            rows = [operand(b, whole(b)) for b in blocks]
            for i in range(first, first + pieces):
                if i not in weights:
                    weights[i] = operand(w_down, pl.BlockSpec((tile, span), lambda n, at, i=i: (n, at[0] ^ i)))
            steps.append((rows, [weights[i] for i in range(first, first + pieces)]))
            work += size * units * pieces * span
            held += 4 * size * pieces * span
        plan.append((of, steps))
        sizes.append(size)
    total = sum(sizes)
    limit = BASE + held + 16 * total * tile
    grid = (units // tile,)
    column = lambda n: pl.BlockSpec((n, tile), lambda n, at: (0, n))
    if coefs is None:
        out = [jax.ShapeDtypeStruct((n, units), F32) for n in sizes]
        kernel = functools.partial(early_kernel, plan)
        return call(
            kernel, "hidden_early", grid, specs, [column(n) for n in sizes], out, [at, *operands], work, limit
        )
    kernel = functools.partial(late_kernel, plan, experts, units // experts, moves)
    outs = [column(total), column(total), pl.BlockSpec((len(moves), more, span), lambda n, at: (0, 0, 0))]
    shapes = [jax.ShapeDtypeStruct((total, units), BF16)] * 2
    shapes.append(jax.ShapeDtypeStruct((len(moves), more, span), BF16))
    return call(
        kernel,
        "hidden_late",
        grid,
        specs + [column(total)] * 3,
        outs,
        shapes,
        [at, *operands, *coefs],
        work,
        limit,
        [pltpu.VMEM((total, 8), F32)],
    )


def expand_kernel(counts, adds, carries, at_ref, ag_ref, au_ref, wg_ref, wu_ref, *refs):
    other, refs = refs[: int(adds)], refs[int(adds) :]
    info, outs = refs[: int(carries)], refs[int(carries) :]
    width = outs[0].shape[3]
    rows = ag_ref.shape[0] // sum(counts)
    tile = tile_of(width)
    for at in range(0, width, tile):
        span = slice(at, at + tile)
        y = jnp.dot(ag_ref[...], wg_ref[:, span], preferred_element_type=F32)
        y = y + jnp.dot(au_ref[...], wu_ref[:, span], preferred_element_type=F32)
        i = 0
        for out, count in zip(outs, counts):
            for j in range(count):
                part = y[i * rows : (i + 1) * rows]
                if adds:
                    part = part + other[0][i, 0, :rows, span].astype(F32)
                out[j, 0, :rows, span] = part.astype(BF16)
                if carries:
                    part = info[0][i, :, span]
                    if adds:
                        part = (part.astype(F32) + other[0][i, 0, rows:, span].astype(F32)).astype(BF16)
                    out[j, 0, rows:, span] = part
                i += 1


def expand(at, first, pieces, part, ag, au, w_gate, w_up, sections, rows, counts, info=None, other=None):
    units = ag.shape[1]
    number = sum(counts)
    span = w_gate.shape[1] // sections
    half = max(span // 2, 128)
    per = span // half
    more = 0 if info is None else info.shape[1]
    some = pl.BlockSpec((number * rows, units), lambda k, j, at: (part, 0))
    weight = pl.BlockSpec((units, half), lambda k, j, at: (0, (at[0] ^ (first + k)) * per + j))
    block = lambda n: pl.BlockSpec((n, 1, rows + more, half), lambda k, j, at: (0, k, 0, j))
    specs, operands = [some, some, weight, weight], [at, ag, au, w_gate, w_up]
    if other is not None:
        specs, operands = specs + [block(number)], operands + [other]
    if info is not None:
        specs.append(pl.BlockSpec((number, more, half), lambda k, j, at: (part, 0, j)))
        operands.append(info)
    return call(
        functools.partial(expand_kernel, counts, other is not None, info is not None),
        "expand",
        (pieces, per),
        specs,
        [block(n) for n in counts],
        [jax.ShapeDtypeStruct((n, pieces, rows + more, span), BF16) for n in counts],
        operands,
        2 * number * rows * units * pieces * span,
        BASE + 8 * number * rows * units + 4 * number * rows * half,
    )


def small(kernel, name, out_shape, operands, specs=None, aliases=None, scratch=(), out_spec=None):
    specs = [pl.BlockSpec(memory_space=pltpu.VMEM)] * len(operands) if specs is None else specs
    return pl.pallas_call(
        kernel,
        in_specs=specs,
        out_specs=pl.BlockSpec(memory_space=pltpu.VMEM) if out_spec is None else out_spec,
        out_shape=out_shape,
        scratch_shapes=scratch,
        input_output_aliases=aliases or {},
        compiler_params=pltpu.CompilerParams(vmem_limit_bytes=BASE),
        cost_estimate=pl.CostEstimate(flops=WEIGHT << 29, bytes_accessed=1 << 20, transcendentals=0),
        name=name,
    )(*operands)


def join_kernel(counts, *refs):
    xs, out, sems = refs[: sum(counts)], refs[-2], refs[-1]
    copies, n = [], 0
    for i, count in enumerate(counts):
        for k in range(count):
            copies.append(pltpu.make_async_copy(xs[n].at[0, 0], out.at[i, k], sems.at[n]))
            n += 1
    for c in copies:
        c.start()
    for c in copies:
        c.wait()


def join(*rows):
    counts = [len(r) for r in rows]
    xs = [x for r in rows for x in r]
    somewhere = pl.BlockSpec(memory_space=pl.ANY)
    return small(
        functools.partial(join_kernel, counts),
        "join",
        jax.ShapeDtypeStruct((len(rows), counts[0], *xs[0].shape[2:]), xs[0].dtype),
        xs,
        specs=[somewhere] * len(xs),
        scratch=[pltpu.SemaphoreType.DMA((len(xs),))],
        out_spec=somewhere,
    )


def pass_on_kernel(two_ref, one_ref, out_ref):
    out_ref[0] = (two_ref[0].astype(F32) + one_ref[0].astype(F32)).astype(BF16)
    out_ref[1] = two_ref[1]


def pass_on(two, one):
    return small(pass_on_kernel, "pass_on", jax.ShapeDtypeStruct(two.shape, BF16), (two, one))


def finish_kernel(a_ref, b_ref, c_ref, out_ref):
    for k in range(out_ref.shape[0]):
        y = a_ref[0, k].astype(F32) + b_ref[0, k].astype(F32) + c_ref[0, k].astype(F32)
        out_ref[k] = y.astype(BF16)


def finish(a, b, c):
    return small(finish_kernel, "finish", jax.ShapeDtypeStruct(a.shape[1:], BF16), (a, b, c))


def add(*terms):
    return functools.reduce(lambda a, b: a + b, [t.astype(F32) for t in terms]).astype(BF16)


def after(x, *others):
    return lax.optimization_barrier((x, *others))[0]


def local(grad_out, probs, expert_ids, w_gate, w_up, w_down, saved_gate, saved_up):
    groups, sections = lax.axis_size("expert"), lax.axis_size("section")
    me, z = lax.axis_index("expert"), lax.axis_index("section")
    experts, units, features = w_gate.shape
    slots = saved_gate.shape[2]
    tokens, topk = expert_ids.shape
    span = grad_out.shape[1]
    square = groups == 8
    flat = lambda w: w.reshape(experts * units, features)
    w_gate, w_up, w_down = flat(w_gate), flat(w_up), flat(w_down)
    core = me % 2
    near = jnp.where(core == 0, 2, 4)
    far = 6 - near

    def swap(x, even, odd):
        return lax.ppermute(x, "expert", [(i, i ^ (even, odd)[i % 2]) for i in range(groups)])

    def across(x, by):
        return lax.ppermute(x, "section", [(i, i ^ by) for i in range(sections)])

    if square:
        owners = jnp.stack([me, me ^ 1, me ^ near, me ^ near ^ 1, me ^ 1 ^ far, me ^ far, me ^ 6, me ^ 7])
        moves = (0, 4, 1, 2, 5, 6, 3, 7)
    else:
        owners, moves = jnp.arange(groups), tuple(range(groups))

    high = lax.reduce_precision(probs, 8, 7)
    routing = jnp.concatenate([expert_ids.T.astype(F32), high.T, (probs - high).T], axis=0)
    lines = 3 * topk
    more = -(-lines * tokens // (16 * span)) * 16
    routing = jnp.pad(routing.reshape(-1), (0, more * span - lines * tokens)).reshape(more, span)
    own = jnp.concatenate([grad_out, routing.astype(BF16)], axis=0)[None, None]
    received = [None] + [across(grad_out[None], i) for i in (1, 2) if i < sections]
    if square:
        pair0 = join([own], [swap(own, 1, 1)])
        first0 = after(swap(pair0, 2, 4), *received[1:3])
        second0 = swap(first0[:1], 4, 2)
        lot0 = [pair0, first0, swap(first0, 1, 1), second0, swap(second0, 1, 1)]
    else:
        first0 = lax.all_gather(own, "expert", axis=0, tiled=True)
        lot0 = [first0]
    for i in range(3, sections):
        received.append(across(after(grad_out[None], received[i - 2]), i))

    at = jnp.concatenate([jnp.stack([z, me * experts]), owners]).astype(jnp.int32)
    gated = lambda at: coefficients(at, lot0, tokens, topk, saved_gate, saved_up, slots // groups)
    if square:
        got = [x[None] for x in received[1:3]]
        pair1 = join(got, [swap(x, 1, 1) for x in got])
        first1 = swap(pair1, 2, 4)
        coefs = gated(after(at, pair1))
        got = [after(x[None], coefs[0]) for x in received[3:]]
        theirs2 = [swap(x, 1, 1) for x in got]
        most, few = hidden(at, [(None, [(0, lot0[:3])]), (None, [(0, lot0[3:])])], tokens, after(w_down, coefs[0]))
        pair2 = join([after(got[0], most), *got[1:]], theirs2)
        first1 = after(first1, pair2)
        second1 = swap(first1[:1], 4, 2)
        first2 = swap(after(pair2, first1), 2, 4)
        lot1 = [pair1, first1, swap(first1, 1, 1)]
        (most,) = hidden(at, [(most, [(1, lot1)])], tokens, w_down)
        second1, first2 = after(second1, most), after(first2, most)
        second2 = swap(first2[:1], 4, 2)
        lot1 = [second1, swap(second1, 1, 1)]
        lot2 = [pair2, first2, swap(first2, 1, 1)], [second2, swap(second2, 1, 1)]
        parts = [(most, [(3, lot2[0])]), (few, [(1, lot1), (3, lot2[1])])]
    else:
        coefs = gated(at)
        gather = lambda xs: [lax.all_gather(jnp.stack(xs, axis=1), "expert", axis=0, tiled=True)]
        (h,) = hidden(at, [(None, [(0, lot0)])], tokens, w_down)
        (h,) = hidden(at, [(h, [(1, gather(received[1:3]))])], tokens, w_down)
        parts = [(h, [(3, gather(received[3:]))])]
    more = -(-2 * groups * experts * tokens // (16 * span)) * 16
    ag, au, info = hidden(at, parts, tokens, w_down, coefs, experts, moves, more)

    lots = ((3, sections), (2, 3), (1, 2), (0, 1))
    half = groups // 2
    last = [info]
    theirs, kept, sent, parts, routers = {}, {}, {}, {}, {}

    def run_expand(n, part, counts, other=None):
        a, b = lots[n]
        outs = expand(
            at, a, b - a, part, after(ag, *last), au, w_gate, w_up, sections, tokens, counts,
            info if n == 0 else None, other,
        )
        last[0] = outs[0]
        return outs

    def theirs_step(n):
        theirs[n] = swap(run_expand(n, 1, (half,))[0], 1, 1)

    def mine_step(n):
        alone, two, one = run_expand(n, 0, (1, 2, 1), theirs[n])
        kept[n] = alone, two, swap(one, 4, 2)

    def sent_step(n):
        _, two, one = kept[n]
        last[0] = pass_on(two, after(one, *last))
        sent[n] = swap(last[0], 2, 4)

    def hand_out(n, sums):
        a = lots[n][0]
        for k, x in enumerate(sums):
            parts[a + k] = x if a + k == 0 else across(x, a + k)
        if n == 0:
            routers[0] = sums[0][tokens:]
            routers.update({i: across(routers[0], i) for i in range(1, 3)})
            for i in range(3, sections):
                routers[i], parts[i] = parts[i][tokens:], parts[i][:tokens]

    def final_step(n):
        mine = sent[n][:1], swap(sent[n][1:], 1, 1)
        last[0] = finish(after(kept[n][0], *last), *mine)
        hand_out(n, list(last[0]))

    if square:
        for step, n in (
            (theirs_step, 0),
            (theirs_step, 1),
            (mine_step, 0),
            (theirs_step, 2),
            (sent_step, 0),
            (mine_step, 1),
            (theirs_step, 3),
            (sent_step, 1),
            (mine_step, 2),
            (final_step, 0),
            (sent_step, 2),
            (mine_step, 3),
            (final_step, 1),
            (sent_step, 3),
            (final_step, 2),
            (final_step, 3),
        ):
            step(n)
    else:
        for n in range(len(lots)):
            outs = run_expand(n, 0, (groups,))
            sums = lax.psum_scatter(outs[0], "expert", scatter_dimension=0, tiled=True)[0]
            hand_out(n, list(sums))
    grad_in = add(*parts.values())

    router = functools.reduce(lambda a, b: a + b, [r.astype(F32) for r in routers.values()])
    count = groups * experts
    router = jnp.sum(router.reshape(-1)[: 2 * count * tokens].reshape(2, count, tokens), axis=0)
    match = expert_ids[None] == jnp.arange(count)[:, None, None]
    grad_probs = jnp.sum(jnp.where(match, router[:, :, None], 0.0), axis=0).astype(BF16)
    return (grad_in, grad_probs)


def solution(mesh):
    placed = (
        P("expert", "section"),
        P("expert", None),
        P("expert", None),
        P("expert", "section", None),
        P("expert", "section", None),
        P("expert", "section", None),
        P("expert", "section", None),
        P("expert", "section", None),
    )
    return jax.shard_map(
        local,
        mesh=mesh,
        in_specs=placed,
        out_specs=(P("expert", "section"), P("expert", None)),
        check_vma=False,
    )
```

```python
import functools

import jax
import jax.numpy as jnp
from jax import lax
from jax.experimental import pallas as pl
from jax.experimental.pallas import tpu as pltpu
from jax.sharding import PartitionSpec as P

F32, BF16 = jnp.float32, jnp.bfloat16
ROWS_BY_ROWS = (((1,), (1,)), ((), ()))
BASE = 10 << 20
WEIGHT = 16


def call(kernel, name, grid, in_specs, out_specs, out_shape, operands, flops, limit, scratch=()):
    outs = out_shape if isinstance(out_shape, list) else [out_shape]
    moved = sum(x.size * x.dtype.itemsize for x in [*operands, *outs])
    return pl.pallas_call(
        kernel,
        grid_spec=pltpu.PrefetchScalarGridSpec(
            num_scalar_prefetch=1,
            grid=grid,
            in_specs=in_specs,
            out_specs=out_specs,
            scratch_shapes=scratch,
        ),
        out_shape=out_shape,
        compiler_params=pltpu.CompilerParams(vmem_limit_bytes=min(limit, 56 << 20)),
        cost_estimate=pl.CostEstimate(flops=WEIGHT * flops, bytes_accessed=moved, transcendentals=0),
        name=name,
    )(*operands)


def coefficient_kernel(capacity, topk, at_ref, info_ref, gate_ref, up_ref, cg_ref, cu_ref, cr_ref, columns_ref):
    experts, width, slots = gate_ref.shape
    blocks, _, tokens = info_ref.shape

    @pl.when(pl.program_id(0) == 0)
    def _():
        before = lax.broadcasted_iota(jnp.int32, (tokens, tokens), 0)
        earlier = (before < lax.broadcasted_iota(jnp.int32, (tokens, tokens), 1)).astype(BF16)
        for b in range(blocks):
            info = info_ref[at_ref[2 + blocks + b]]
            ids, prob = info[:topk], info[topk:]
            named, weight = [], []
            for e in range(experts):
                chosen = ids == (at_ref[1] + e).astype(F32)
                named.append(jnp.max(jnp.where(chosen, 1.0, 0.0), axis=0, keepdims=True))
                weight.append(jnp.sum(jnp.where(chosen, prob, 0.0), axis=0, keepdims=True))
            named = jnp.concatenate(named, axis=0)
            position = jnp.dot(named.astype(BF16), earlier, preferred_element_type=F32)
            slot = jnp.where(named > 0.0, position + (at_ref[2 + b] * capacity).astype(F32), -1.0)
            fill = jnp.zeros((8 - 2 * experts, tokens), F32)
            columns_ref[b * tokens : (b + 1) * tokens] = jnp.transpose(
                jnp.concatenate([slot, *weight, fill], axis=0)
            )

    rows = cg_ref.shape[0]
    columns = columns_ref[pl.ds(pl.multiple_of(pl.program_id(0) * rows, rows), rows)]
    number = lax.broadcasted_iota(jnp.int32, (rows, slots), 1).astype(F32)
    for e in range(experts):
        pick = jnp.where(columns[:, e : e + 1] == number, 1.0, 0.0).astype(BF16)
        g = lax.dot_general(pick, gate_ref[e], ROWS_BY_ROWS, preferred_element_type=F32)
        u = lax.dot_general(pick, up_ref[e], ROWS_BY_ROWS, preferred_element_type=F32)
        p = columns[:, experts + e : experts + e + 1]
        sg = 1.0 / (1.0 + jnp.exp(-g))
        silu = g * sg
        span = slice(e * width, (e + 1) * width)
        cg_ref[:, span] = (u * sg * (1.0 + g * (1.0 - sg)) * p).astype(BF16)
        cu_ref[:, span] = (silu * p).astype(BF16)
        cr_ref[:, span] = (silu * u).astype(BF16)


def coefficients(at, info, topk, saved_gate, saved_up, capacity):
    experts, width, slots = saved_gate.shape
    blocks, _, tokens = info.shape
    tile = (4 if blocks % 4 == 0 else 1) * tokens
    total = blocks * tokens
    whole = lambda x: pl.BlockSpec(x.shape, lambda i, at: (0, 0, 0))
    out = pl.BlockSpec((tile, experts * width), lambda i, at: (i, 0))
    return call(
        functools.partial(coefficient_kernel, capacity, topk),
        "coefficients",
        (total // tile,),
        [whole(info), whole(saved_gate), whole(saved_up)],
        [out] * 3,
        [jax.ShapeDtypeStruct((total, experts * width), BF16)] * 3,
        (at, info, saved_gate, saved_up),
        4 * total * slots * experts * width,
        2 * BASE,
        [pltpu.VMEM((total, 8), F32)],
    )


def products(plan, refs):
    sums = []
    for before, lots in plan:
        total = None if before is None else refs[before][...]
        for blocks, weights in lots:
            for k, weight in enumerate(weights):
                xs = [refs[i][:, k] for i in blocks]
                xs = [x.reshape(x.shape[0] * x.shape[1], x.shape[2]) for x in xs]
                x = xs[0] if len(xs) == 1 else jnp.concatenate(xs, axis=0)
                y = lax.dot_general(x, refs[weight][...], ROWS_BY_ROWS, preferred_element_type=F32)
                total = y if total is None else total + y
        sums.append(total)
    return sums


def early_kernel(plan, at_ref, *refs):
    for out_ref, h in zip(refs[len(refs) - len(plan) :], products(plan, refs)):
        out_ref[...] = h


def late_kernel(plan, experts, width, moves, at_ref, *refs):
    cg_ref, cu_ref, cr_ref, ag_ref, au_ref, info_ref, r_ref = refs[len(refs) - 7 :]
    total, tile = ag_ref.shape
    tokens = total // len(moves)

    @pl.when(pl.program_id(0) == 0)
    def _():
        r_ref[...] = jnp.zeros_like(r_ref)

    at = 0
    for h in products(plan, refs):
        rows = slice(at, at + h.shape[0])
        ag = (h * cg_ref[rows].astype(F32)).astype(BF16)
        au = (h * cu_ref[rows].astype(F32)).astype(BF16)
        terms = h * cr_ref[rows].astype(F32)
        for i in range(h.shape[0] // tokens):
            j = moves[at // tokens + i]
            to, of = slice(j * tokens, (j + 1) * tokens), slice(i * tokens, (i + 1) * tokens)
            ag_ref[to], au_ref[to] = ag[of], au[of]
        unit = pl.program_id(0) * tile + lax.broadcasted_iota(jnp.int32, terms.shape, 1)
        for e in range(experts):
            own = (unit >= e * width) & (unit < (e + 1) * width)
            r_ref[rows, e : e + 1] += jnp.sum(jnp.where(own, terms, 0.0), axis=1, keepdims=True)
        at += h.shape[0]

    @pl.when(pl.program_id(0) == pl.num_programs(0) - 1)
    def _():
        more, span = info_ref.shape[1:]
        per, count = span // tokens, experts * len(moves)
        for i, j in enumerate(moves):
            value = jnp.transpose(r_ref[i * tokens : (i + 1) * tokens])
            high = value.astype(BF16).astype(F32)
            parts = []
            for x in (high, value - high):
                for n in range(count):
                    own = [jnp.where(at_ref[1] + e == n, x[e : e + 1], 0.0) for e in range(experts)]
                    parts.append(functools.reduce(lambda p, q: p + q, own))
            parts += [jnp.zeros((1, tokens), F32)] * (more * per - len(parts))
            lines = [jnp.concatenate(parts[n : n + per], axis=1) for n in range(0, more * per, per)]
            info_ref[j] = jnp.concatenate(lines, axis=0).astype(BF16)


def tile_of(n):
    return 256 if n % 256 == 0 else 128 if n % 128 == 0 else n


def hidden(at, parts, tokens, w_down, coefs=None, experts=None, moves=None, more=None):
    units = w_down.shape[0]
    tile = tile_of(units)
    specs, operands, weights, plan, sizes, work, held = [], [], {}, [], [], 0, 0

    def operand(x, spec):
        operands.append(x)
        specs.append(spec)
        return len(operands) - 1

    for before, lots in parts:
        size = tokens * sum(b.shape[0] for b in lots[0][1])
        of = None
        if before is not None:
            of = operand(before, pl.BlockSpec((size, tile), lambda n, at: (0, n)))
        steps = []
        for first, blocks in lots:
            pieces, span = blocks[0].shape[1], blocks[0].shape[3]
            whole = lambda b: pl.BlockSpec((b.shape[0], pieces, tokens, span), lambda n, at: (0, 0, 0, 0))
            rows = [operand(b, whole(b)) for b in blocks]
            for i in range(first, first + pieces):
                if i not in weights:
                    weights[i] = operand(w_down, pl.BlockSpec((tile, span), lambda n, at, i=i: (n, at[0] ^ i)))
            steps.append((rows, [weights[i] for i in range(first, first + pieces)]))
            work += size * units * pieces * span
            held += 4 * size * pieces * span
        plan.append((of, steps))
        sizes.append(size)
    total = sum(sizes)
    limit = BASE + held + 16 * total * tile
    grid = (units // tile,)
    column = lambda n: pl.BlockSpec((n, tile), lambda n, at: (0, n))
    if coefs is None:
        out = [jax.ShapeDtypeStruct((n, units), F32) for n in sizes]
        kernel = functools.partial(early_kernel, plan)
        return call(
            kernel, "hidden_early", grid, specs, [column(n) for n in sizes], out, [at, *operands], work, limit
        )
    kernel = functools.partial(late_kernel, plan, experts, units // experts, moves)
    outs = [column(total), column(total), pl.BlockSpec((len(moves), more, span), lambda n, at: (0, 0, 0))]
    shapes = [jax.ShapeDtypeStruct((total, units), BF16)] * 2
    shapes.append(jax.ShapeDtypeStruct((len(moves), more, span), BF16))
    return call(
        kernel,
        "hidden_late",
        grid,
        specs + [column(total)] * 3,
        outs,
        shapes,
        [at, *operands, *coefs],
        work,
        limit,
        [pltpu.VMEM((total, 8), F32)],
    )


def expand_kernel(counts, adds, carries, at_ref, ag_ref, au_ref, wg_ref, wu_ref, *refs):
    other, refs = refs[: int(adds)], refs[int(adds) :]
    info, outs = refs[: int(carries)], refs[int(carries) :]
    width = outs[0].shape[3]
    rows = ag_ref.shape[0] // sum(counts)
    tile = tile_of(width)
    for at in range(0, width, tile):
        span = slice(at, at + tile)
        y = jnp.dot(ag_ref[...], wg_ref[:, span], preferred_element_type=F32)
        y = y + jnp.dot(au_ref[...], wu_ref[:, span], preferred_element_type=F32)
        i = 0
        for out, count in zip(outs, counts):
            for j in range(count):
                part = y[i * rows : (i + 1) * rows]
                if adds:
                    part = part + other[0][i, 0, :rows, span].astype(F32)
                out[j, 0, :rows, span] = part.astype(BF16)
                if carries:
                    part = info[0][i, :, span]
                    if adds:
                        part = (part.astype(F32) + other[0][i, 0, rows:, span].astype(F32)).astype(BF16)
                    out[j, 0, rows:, span] = part
                i += 1


def expand(at, first, pieces, part, ag, au, w_gate, w_up, sections, rows, counts, info=None, other=None):
    units = ag.shape[1]
    number = sum(counts)
    span = w_gate.shape[1] // sections
    half = max(span // 2, 128)
    per = span // half
    more = 0 if info is None else info.shape[1]
    some = pl.BlockSpec((number * rows, units), lambda k, j, at: (part, 0))
    weight = pl.BlockSpec((units, half), lambda k, j, at: (0, (at[0] ^ (first + k)) * per + j))
    block = lambda n: pl.BlockSpec((n, 1, rows + more, half), lambda k, j, at: (0, k, 0, j))
    specs, operands = [some, some, weight, weight], [at, ag, au, w_gate, w_up]
    if other is not None:
        specs, operands = specs + [block(number)], operands + [other]
    if info is not None:
        specs.append(pl.BlockSpec((number, more, half), lambda k, j, at: (part, 0, j)))
        operands.append(info)
    return call(
        functools.partial(expand_kernel, counts, other is not None, info is not None),
        "expand",
        (pieces, per),
        specs,
        [block(n) for n in counts],
        [jax.ShapeDtypeStruct((n, pieces, rows + more, span), BF16) for n in counts],
        operands,
        2 * number * rows * units * pieces * span,
        BASE + 8 * number * rows * units + 4 * number * rows * half,
    )


def small(kernel, name, out_shape, operands, specs=None, scratch=(), out_spec=None, flops=1 << 30):
    specs = [pl.BlockSpec(memory_space=pltpu.VMEM)] * len(operands) if specs is None else specs
    return pl.pallas_call(
        kernel,
        in_specs=specs,
        out_specs=pl.BlockSpec(memory_space=pltpu.VMEM) if out_spec is None else out_spec,
        out_shape=out_shape,
        scratch_shapes=scratch,
        compiler_params=pltpu.CompilerParams(vmem_limit_bytes=BASE),
        cost_estimate=pl.CostEstimate(flops=flops, bytes_accessed=0, transcendentals=0),
        name=name,
    )(*operands)


def join_kernel(counts, *refs):
    xs, out, sems = refs[: sum(counts)], refs[-2], refs[-1]
    copies, n = [], 0
    for i, count in enumerate(counts):
        for k in range(count):
            copies.append(pltpu.make_async_copy(xs[n].at[0, 0], out.at[i, k], sems.at[n]))
            n += 1
    for c in copies:
        c.start()
    for c in copies:
        c.wait()


def join(*rows):
    counts = [len(r) for r in rows]
    xs = [x for r in rows for x in r]
    somewhere = pl.BlockSpec(memory_space=pl.ANY)
    return small(
        functools.partial(join_kernel, counts),
        "join",
        jax.ShapeDtypeStruct((len(rows), counts[0], *xs[0].shape[2:]), xs[0].dtype),
        xs,
        specs=[somewhere] * len(xs),
        scratch=[pltpu.SemaphoreType.DMA((len(xs),))],
        out_spec=somewhere,
        flops=0,
    )


def pass_on_kernel(two_ref, one_ref, out_ref):
    out_ref[0] = (two_ref[0].astype(F32) + one_ref[0].astype(F32)).astype(BF16)
    out_ref[1] = two_ref[1]


def pass_on(two, one):
    return small(pass_on_kernel, "pass_on", jax.ShapeDtypeStruct(two.shape, BF16), (two, one))


def finish_kernel(a_ref, b_ref, c_ref, *refs):
    extra, out_ref = refs[:-1], refs[-1]
    rows = a_ref.shape[2]
    for k in range(out_ref.shape[0]):
        y = a_ref[0, k].astype(F32) + b_ref[0, k].astype(F32) + c_ref[0, k].astype(F32)
        out_ref[k, :rows] = y.astype(BF16)
        if extra:
            out_ref[k, rows:] = extra[0][...]


def finish(a, b, c, *extra):
    more = extra[0].shape[0] if extra else 0
    shape = (a.shape[1], a.shape[2] + more, a.shape[3])
    return small(finish_kernel, "finish", jax.ShapeDtypeStruct(shape, BF16), (a, b, c, *extra))


def add(*terms):
    return functools.reduce(lambda a, b: a + b, [t.astype(F32) for t in terms]).astype(BF16)


def after(x, *others):
    return lax.optimization_barrier((x, *others))[0]


def local(grad_out, probs, expert_ids, w_gate, w_up, w_down, saved_gate, saved_up):
    groups, sections = lax.axis_size("expert"), lax.axis_size("section")
    me, z = lax.axis_index("expert"), lax.axis_index("section")
    experts, units, features = w_gate.shape
    slots = saved_gate.shape[2]
    tokens, topk = expert_ids.shape
    span = grad_out.shape[1]
    square = groups == 8
    flat = lambda w: w.reshape(experts * units, features)
    w_gate, w_up, w_down = flat(w_gate), flat(w_up), flat(w_down)
    core = me % 2
    near = jnp.where(core == 0, 2, 4)
    far = 6 - near

    def swap(x, even, odd):
        return lax.ppermute(x, "expert", [(i, i ^ (even, odd)[i % 2]) for i in range(groups)])

    def across(x, by):
        return lax.ppermute(x, "section", [(i, i ^ by) for i in range(sections)])

    if square:
        owners = jnp.stack([me, me ^ 1, me ^ near, me ^ near ^ 1, me ^ 1 ^ far, me ^ far, me ^ 6, me ^ 7])
        moves = (0, 4, 1, 2, 5, 6, 3, 7)
    else:
        owners, moves = jnp.arange(groups), tuple(range(groups))

    piece = grad_out[None, None]
    received = [piece] + [across(piece, i) for i in (1, 2) if i < sections]
    for i in range(3, sections):
        received.append(across(after(piece, *received[1:3]), i))
    info = jnp.concatenate([expert_ids.T.astype(F32), probs.T], axis=0)[None]
    if square:
        for bit in (2, 4, 1):
            info = jnp.concatenate([info, swap(info, bit, bit)], axis=0)
        place = owners ^ me
        place = place // 2 + place % 2 * 4
    else:
        info = lax.all_gather(info, "expert", axis=0, tiled=True)
        place = owners
    at = jnp.concatenate([jnp.stack([z, me * experts]), owners, place]).astype(jnp.int32)
    gated = lambda at: coefficients(at, info, topk, saved_gate, saved_up, slots // groups)
    if square:
        sibs = [swap(x, 1, 1) for x in received[:3]]
        pair1 = join([after(piece, info), *received[1:3]], sibs)
        first1 = swap(pair1, 2, 4)
        coefs = gated(after(at, pair1))
        got = [after(x, coefs[0]) for x in received[3:]]
        pair2 = join(got, [swap(x, 1, 1) for x in got])
        first1 = after(first1, pair2)
        second1 = swap(first1[:1], 4, 2)
        first2 = swap(after(pair2, first1), 2, 4)
        lot1 = [pair1, first1, swap(first1, 1, 1)]
        (most,) = hidden(at, [(None, [(0, lot1)])], tokens, after(w_down, coefs[0]))
        second1, first2, _ = lax.optimization_barrier((second1, first2, most))
        second2 = swap(first2[:1], 4, 2)
        lot1 = [second1, swap(second1, 1, 1)]
        (few,) = hidden(at, [(None, [(0, lot1)])], tokens, w_down)
        second2 = after(second2, few)
        lot2 = [pair2, first2, swap(first2, 1, 1)], [second2, swap(second2, 1, 1)]
        parts = [(most, [(3, lot2[0])]), (few, [(3, lot2[1])])]
    else:
        coefs = gated(at)
        gather = lambda xs: [lax.all_gather(jnp.concatenate(xs, axis=1), "expert", axis=0, tiled=True)]
        (h,) = hidden(at, [(None, [(0, gather(received[:3]))])], tokens, w_down)
        parts = [(h, [(3, gather(received[3:]))])]
    more = -(-2 * groups * experts * tokens // (16 * span)) * 16
    ag, au, info = hidden(at, parts, tokens, w_down, coefs, experts, moves, more)

    lots = ((3, sections), (2, 3), (1, 2), (0, 1))
    half = groups // 2
    last = [info]
    theirs, kept, sent, parts, routers = {}, {}, {}, {}, {}

    def run_expand(n, part, counts, other=None):
        a, b = lots[n]
        outs = expand(
            at, a, b - a, part, after(ag, *last), au, w_gate, w_up, sections, tokens, counts,
            info if n == 0 else None, other,
        )
        last[0] = outs[0]
        return outs

    def theirs_step(n):
        theirs[n] = swap(run_expand(n, 1, (half,))[0], 1, 1)

    def mine_step(n):
        alone, two, one = run_expand(n, 0, (1, 2, 1), theirs[n])
        kept[n] = alone, two, swap(one, 4, 2)

    def sent_step(n):
        _, two, one = kept[n]
        last[0] = pass_on(two, after(one, *last))
        sent[n] = swap(last[0], 2, 4)

    def hand_out(n, sums):
        a = lots[n][0]
        for k, x in enumerate(sums):
            if a + k == 0:
                parts[0] = x
                continue
            if n == 0 and k == 0:
                routers[0] = x[tokens:]
            x = across(x, a + k)
            parts[a + k] = x[:tokens]
            if n == 0:
                routers[a + k] = x[tokens:]
        if n == 0:
            routers.update({i: across(routers[0], i) for i in range(1, 3) if i < sections})

    def receive_step(n):
        got = after(sent[n], *last)
        sent[n] = got[:1], swap(got[1:], 1, 1)

    def final_step(n):
        last[0] = finish(after(kept[n][0], *last), *sent[n])
        hand_out(n, list(last[0]))

    if square:
        for step, n in (
            (theirs_step, 0),
            (theirs_step, 1),
            (mine_step, 0),
            (mine_step, 1),
            (sent_step, 0),
            (theirs_step, 2),
            (theirs_step, 3),
            (sent_step, 1),
            (mine_step, 2),
            (mine_step, 3),
            (receive_step, 0),
            (sent_step, 2),
            (final_step, 0),
            (receive_step, 1),
            (final_step, 1),
            (receive_step, 2),
            (sent_step, 3),
            (receive_step, 3),
            (final_step, 2),
            (final_step, 3),
        ):
            step(n)
    else:
        for n, (a, b) in enumerate(lots):
            outs = run_expand(n, 0, (groups,))
            sums = lax.psum_scatter(outs[0], "expert", scatter_dimension=0, tiled=True)[0]
            hand_out(n, list(sums))
    grad_in = add(*parts.values())

    router = functools.reduce(lambda a, b: a + b, [r.astype(F32) for r in routers.values()])
    count = groups * experts
    router = jnp.sum(router.reshape(-1)[: 2 * count * tokens].reshape(2, count, tokens), axis=0)
    match = expert_ids[None] == jnp.arange(count)[:, None, None]
    grad_probs = jnp.sum(jnp.where(match, router[:, :, None], 0.0), axis=0).astype(BF16)
    return (grad_in, grad_probs)


def solution(mesh):
    placed = (
        P("expert", "section"),
        P("expert", None),
        P("expert", None),
        P("expert", "section", None),
        P("expert", "section", None),
        P("expert", "section", None),
        P("expert", "section", None),
        P("expert", "section", None),
    )
    return jax.shard_map(
        local,
        mesh=mesh,
        in_specs=placed,
        out_specs=(P("expert", "section"), P("expert", None)),
        check_vma=False,
    )
```

```python
import functools

import jax
import jax.numpy as jnp
from jax import lax
from jax.experimental import pallas as pl
from jax.experimental.pallas import tpu as pltpu
from jax.sharding import PartitionSpec as P

F32, BF16 = jnp.float32, jnp.bfloat16
ROWS_BY_ROWS = (((1,), (1,)), ((), ()))
BASE = 10 << 20
WEIGHT = 16


def call(kernel, name, grid, in_specs, out_specs, out_shape, operands, flops, limit, scratch=()):
    outs = out_shape if isinstance(out_shape, list) else [out_shape]
    moved = sum(x.size * x.dtype.itemsize for x in [*operands, *outs])
    return pl.pallas_call(
        kernel,
        grid_spec=pltpu.PrefetchScalarGridSpec(
            num_scalar_prefetch=1,
            grid=grid,
            in_specs=in_specs,
            out_specs=out_specs,
            scratch_shapes=scratch,
        ),
        out_shape=out_shape,
        compiler_params=pltpu.CompilerParams(vmem_limit_bytes=min(limit, 56 << 20)),
        cost_estimate=pl.CostEstimate(flops=WEIGHT * flops, bytes_accessed=moved, transcendentals=0),
        name=name,
    )(*operands)


def coefficient_kernel(capacity, topk, at_ref, info_ref, gate_ref, up_ref, cg_ref, cu_ref, cr_ref, columns_ref):
    experts, width, slots = gate_ref.shape
    blocks, _, tokens = info_ref.shape

    @pl.when(pl.program_id(0) == 0)
    def _():
        before = lax.broadcasted_iota(jnp.int32, (tokens, tokens), 0)
        earlier = (before < lax.broadcasted_iota(jnp.int32, (tokens, tokens), 1)).astype(BF16)
        for b in range(blocks):
            info = info_ref[at_ref[2 + blocks + b]]
            ids, prob = info[:topk], info[topk:]
            named, weight = [], []
            for e in range(experts):
                chosen = ids == (at_ref[1] + e).astype(F32)
                named.append(jnp.max(jnp.where(chosen, 1.0, 0.0), axis=0, keepdims=True))
                weight.append(jnp.sum(jnp.where(chosen, prob, 0.0), axis=0, keepdims=True))
            named = jnp.concatenate(named, axis=0)
            position = jnp.dot(named.astype(BF16), earlier, preferred_element_type=F32)
            slot = jnp.where(named > 0.0, position + (at_ref[2 + b] * capacity).astype(F32), -1.0)
            fill = jnp.zeros((8 - 2 * experts, tokens), F32)
            columns_ref[b * tokens : (b + 1) * tokens] = jnp.transpose(
                jnp.concatenate([slot, *weight, fill], axis=0)
            )

    rows = cg_ref.shape[0]
    columns = columns_ref[pl.ds(pl.multiple_of(pl.program_id(0) * rows, rows), rows)]
    number = lax.broadcasted_iota(jnp.int32, (rows, slots), 1).astype(F32)
    for e in range(experts):
        pick = jnp.where(columns[:, e : e + 1] == number, 1.0, 0.0).astype(BF16)
        g = lax.dot_general(pick, gate_ref[e], ROWS_BY_ROWS, preferred_element_type=F32)
        u = lax.dot_general(pick, up_ref[e], ROWS_BY_ROWS, preferred_element_type=F32)
        p = columns[:, experts + e : experts + e + 1]
        sg = 1.0 / (1.0 + jnp.exp(-g))
        silu = g * sg
        span = slice(e * width, (e + 1) * width)
        cg_ref[:, span] = (u * sg * (1.0 + g * (1.0 - sg)) * p).astype(BF16)
        cu_ref[:, span] = (silu * p).astype(BF16)
        cr_ref[:, span] = (silu * u).astype(BF16)


def coefficients(at, info, topk, saved_gate, saved_up, capacity):
    experts, width, slots = saved_gate.shape
    blocks, _, tokens = info.shape
    tile = (4 if blocks % 4 == 0 else 1) * tokens
    total = blocks * tokens
    whole = lambda x: pl.BlockSpec(x.shape, lambda i, at: (0, 0, 0))
    out = pl.BlockSpec((tile, experts * width), lambda i, at: (i, 0))
    return call(
        functools.partial(coefficient_kernel, capacity, topk),
        "coefficients",
        (total // tile,),
        [whole(info), whole(saved_gate), whole(saved_up)],
        [out] * 3,
        [jax.ShapeDtypeStruct((total, experts * width), BF16)] * 3,
        (at, info, saved_gate, saved_up),
        4 * total * slots * experts * width,
        2 * BASE,
        [pltpu.VMEM((total, 8), F32)],
    )


def products(plan, refs):
    sums = []
    for before, lots in plan:
        total = None if before is None else refs[before][...]
        for blocks, weights in lots:
            for k, weight in enumerate(weights):
                xs = [refs[i][:, k] for i in blocks]
                xs = [x.reshape(x.shape[0] * x.shape[1], x.shape[2]) for x in xs]
                x = xs[0] if len(xs) == 1 else jnp.concatenate(xs, axis=0)
                y = lax.dot_general(x, refs[weight][...], ROWS_BY_ROWS, preferred_element_type=F32)
                total = y if total is None else total + y
        sums.append(total)
    return sums


def early_kernel(plan, at_ref, *refs):
    for out_ref, h in zip(refs[len(refs) - len(plan) :], products(plan, refs)):
        out_ref[...] = h


def late_kernel(plan, experts, width, moves, at_ref, *refs):
    cg_ref, cu_ref, cr_ref, ag_ref, au_ref, info_ref, r_ref = refs[len(refs) - 7 :]
    total, tile = ag_ref.shape
    tokens = total // len(moves)

    @pl.when(pl.program_id(0) == 0)
    def _():
        r_ref[...] = jnp.zeros_like(r_ref)

    at = 0
    for h in products(plan, refs):
        rows = slice(at, at + h.shape[0])
        ag = (h * cg_ref[rows].astype(F32)).astype(BF16)
        au = (h * cu_ref[rows].astype(F32)).astype(BF16)
        terms = h * cr_ref[rows].astype(F32)
        for i in range(h.shape[0] // tokens):
            j = moves[at // tokens + i]
            to, of = slice(j * tokens, (j + 1) * tokens), slice(i * tokens, (i + 1) * tokens)
            ag_ref[to], au_ref[to] = ag[of], au[of]
        unit = pl.program_id(0) * tile + lax.broadcasted_iota(jnp.int32, terms.shape, 1)
        for e in range(experts):
            own = (unit >= e * width) & (unit < (e + 1) * width)
            r_ref[rows, e : e + 1] += jnp.sum(jnp.where(own, terms, 0.0), axis=1, keepdims=True)
        at += h.shape[0]

    @pl.when(pl.program_id(0) == pl.num_programs(0) - 1)
    def _():
        more, span = info_ref.shape[1:]
        per, count = span // tokens, experts * len(moves)
        for i, j in enumerate(moves):
            value = jnp.transpose(r_ref[i * tokens : (i + 1) * tokens])
            high = value.astype(BF16).astype(F32)
            parts = []
            for x in (high, value - high):
                for n in range(count):
                    own = [jnp.where(at_ref[1] + e == n, x[e : e + 1], 0.0) for e in range(experts)]
                    parts.append(functools.reduce(lambda p, q: p + q, own))
            parts += [jnp.zeros((1, tokens), F32)] * (more * per - len(parts))
            lines = [jnp.concatenate(parts[n : n + per], axis=1) for n in range(0, more * per, per)]
            info_ref[j] = jnp.concatenate(lines, axis=0).astype(BF16)


def tile_of(n):
    return 256 if n % 256 == 0 else 128 if n % 128 == 0 else n


def hidden(at, parts, tokens, w_down, coefs=None, experts=None, moves=None, more=None):
    units = w_down.shape[0]
    tile = tile_of(units)
    specs, operands, weights, plan, sizes, work, held = [], [], {}, [], [], 0, 0

    def operand(x, spec):
        operands.append(x)
        specs.append(spec)
        return len(operands) - 1

    for before, lots in parts:
        size = tokens * sum(b.shape[0] for b in lots[0][1])
        of = None
        if before is not None:
            of = operand(before, pl.BlockSpec((size, tile), lambda n, at: (0, n)))
        steps = []
        for first, blocks in lots:
            pieces, span = blocks[0].shape[1], blocks[0].shape[3]
            whole = lambda b: pl.BlockSpec((b.shape[0], pieces, tokens, span), lambda n, at: (0, 0, 0, 0))
            rows = [operand(b, whole(b)) for b in blocks]
            for i in range(first, first + pieces):
                if i not in weights:
                    weights[i] = operand(w_down, pl.BlockSpec((tile, span), lambda n, at, i=i: (n, at[0] ^ i)))
            steps.append((rows, [weights[i] for i in range(first, first + pieces)]))
            work += size * units * pieces * span
            held += 4 * size * pieces * span
        plan.append((of, steps))
        sizes.append(size)
    total = sum(sizes)
    limit = BASE + held + 16 * total * tile
    grid = (units // tile,)
    column = lambda n: pl.BlockSpec((n, tile), lambda n, at: (0, n))
    if coefs is None:
        out = [jax.ShapeDtypeStruct((n, units), F32) for n in sizes]
        kernel = functools.partial(early_kernel, plan)
        return call(
            kernel, "hidden_early", grid, specs, [column(n) for n in sizes], out, [at, *operands], work, limit
        )
    kernel = functools.partial(late_kernel, plan, experts, units // experts, moves)
    outs = [column(total), column(total), pl.BlockSpec((len(moves), more, span), lambda n, at: (0, 0, 0))]
    shapes = [jax.ShapeDtypeStruct((total, units), BF16)] * 2
    shapes.append(jax.ShapeDtypeStruct((len(moves), more, span), BF16))
    return call(
        kernel,
        "hidden_late",
        grid,
        specs + [column(total)] * 3,
        outs,
        shapes,
        [at, *operands, *coefs],
        work,
        limit,
        [pltpu.VMEM((total, 8), F32)],
    )


def expand_kernel(counts, adds, carries, at_ref, ag_ref, au_ref, wg_ref, wu_ref, *refs):
    other, refs = refs[: int(adds)], refs[int(adds) :]
    info, outs = refs[: int(carries)], refs[int(carries) :]
    width = outs[0].shape[3]
    rows = ag_ref.shape[0] // sum(counts)
    tile = tile_of(width)
    for at in range(0, width, tile):
        span = slice(at, at + tile)
        y = jnp.dot(ag_ref[...], wg_ref[:, span], preferred_element_type=F32)
        y = y + jnp.dot(au_ref[...], wu_ref[:, span], preferred_element_type=F32)
        i = 0
        for out, count in zip(outs, counts):
            for j in range(count):
                part = y[i * rows : (i + 1) * rows]
                if adds:
                    part = part + other[0][i, 0, :rows, span].astype(F32)
                out[j, 0, :rows, span] = part.astype(BF16)
                if carries:
                    part = info[0][i, :, span]
                    if adds:
                        part = (part.astype(F32) + other[0][i, 0, rows:, span].astype(F32)).astype(BF16)
                    out[j, 0, rows:, span] = part
                i += 1


def expand(at, first, pieces, part, ag, au, w_gate, w_up, sections, rows, counts, info=None, other=None):
    units = ag.shape[1]
    number = sum(counts)
    span = w_gate.shape[1] // sections
    half = max(span // 2, 128)
    per = span // half
    more = 0 if info is None else info.shape[1]
    some = pl.BlockSpec((number * rows, units), lambda k, j, at: (part, 0))
    weight = pl.BlockSpec((units, half), lambda k, j, at: (0, (at[0] ^ (first + k)) * per + j))
    block = lambda n: pl.BlockSpec((n, 1, rows + more, half), lambda k, j, at: (0, k, 0, j))
    specs, operands = [some, some, weight, weight], [at, ag, au, w_gate, w_up]
    if other is not None:
        specs, operands = specs + [block(number)], operands + [other]
    if info is not None:
        specs.append(pl.BlockSpec((number, more, half), lambda k, j, at: (part, 0, j)))
        operands.append(info)
    return call(
        functools.partial(expand_kernel, counts, other is not None, info is not None),
        "expand",
        (pieces, per),
        specs,
        [block(n) for n in counts],
        [jax.ShapeDtypeStruct((n, pieces, rows + more, span), BF16) for n in counts],
        operands,
        2 * number * rows * units * pieces * span,
        BASE + 8 * number * rows * units + 4 * number * rows * half,
    )


def small(kernel, name, out_shape, operands, specs=None, scratch=(), out_spec=None, flops=1 << 30):
    specs = [pl.BlockSpec(memory_space=pltpu.VMEM)] * len(operands) if specs is None else specs
    return pl.pallas_call(
        kernel,
        in_specs=specs,
        out_specs=pl.BlockSpec(memory_space=pltpu.VMEM) if out_spec is None else out_spec,
        out_shape=out_shape,
        scratch_shapes=scratch,
        compiler_params=pltpu.CompilerParams(vmem_limit_bytes=BASE),
        cost_estimate=pl.CostEstimate(flops=flops, bytes_accessed=0, transcendentals=0),
        name=name,
    )(*operands)


def join_kernel(counts, *refs):
    xs, out, sems = refs[: sum(counts)], refs[-2], refs[-1]
    copies, n = [], 0
    for i, count in enumerate(counts):
        for k in range(count):
            copies.append(pltpu.make_async_copy(xs[n].at[0, 0], out.at[i, k], sems.at[n]))
            n += 1
    for c in copies:
        c.start()
    for c in copies:
        c.wait()


def join(*rows):
    counts = [len(r) for r in rows]
    xs = [x for r in rows for x in r]
    somewhere = pl.BlockSpec(memory_space=pl.ANY)
    return small(
        functools.partial(join_kernel, counts),
        "join",
        jax.ShapeDtypeStruct((len(rows), counts[0], *xs[0].shape[2:]), xs[0].dtype),
        xs,
        specs=[somewhere] * len(xs),
        scratch=[pltpu.SemaphoreType.DMA((len(xs),))],
        out_spec=somewhere,
        flops=0,
    )


def pass_on_kernel(two_ref, one_ref, out_ref):
    out_ref[0] = (two_ref[0].astype(F32) + one_ref[0].astype(F32)).astype(BF16)
    out_ref[1] = two_ref[1]


def pass_on(two, one):
    return small(pass_on_kernel, "pass_on", jax.ShapeDtypeStruct(two.shape, BF16), (two, one))


def finish_kernel(a_ref, b_ref, c_ref, *refs):
    extra, out_ref = refs[:-1], refs[-1]
    rows = a_ref.shape[2]
    for k in range(out_ref.shape[0]):
        y = a_ref[0, k].astype(F32) + b_ref[0, k].astype(F32) + c_ref[0, k].astype(F32)
        out_ref[k, :rows] = y.astype(BF16)
        if extra:
            out_ref[k, rows:] = extra[0][...]


def finish(a, b, c, *extra):
    more = extra[0].shape[0] if extra else 0
    shape = (a.shape[1], a.shape[2] + more, a.shape[3])
    return small(finish_kernel, "finish", jax.ShapeDtypeStruct(shape, BF16), (a, b, c, *extra))


def add(*terms):
    return functools.reduce(lambda a, b: a + b, [t.astype(F32) for t in terms]).astype(BF16)


def after(x, *others):
    return lax.optimization_barrier((x, *others))[0]


def local(grad_out, probs, expert_ids, w_gate, w_up, w_down, saved_gate, saved_up):
    groups, sections = lax.axis_size("expert"), lax.axis_size("section")
    me, z = lax.axis_index("expert"), lax.axis_index("section")
    experts, units, features = w_gate.shape
    slots = saved_gate.shape[2]
    tokens, topk = expert_ids.shape
    span = grad_out.shape[1]
    square = groups == 8
    flat = lambda w: w.reshape(experts * units, features)
    w_gate, w_up, w_down = flat(w_gate), flat(w_up), flat(w_down)
    core = me % 2
    near = jnp.where(core == 0, 2, 4)
    far = 6 - near

    def swap(x, even, odd):
        return lax.ppermute(x, "expert", [(i, i ^ (even, odd)[i % 2]) for i in range(groups)])

    def across(x, by):
        return lax.ppermute(x, "section", [(i, i ^ by) for i in range(sections)])

    if square:
        owners = jnp.stack([me, me ^ 1, me ^ near, me ^ near ^ 1, me ^ 1 ^ far, me ^ far, me ^ 6, me ^ 7])
        moves = (0, 4, 1, 2, 5, 6, 3, 7)
    else:
        owners, moves = jnp.arange(groups), tuple(range(groups))

    piece = grad_out[None, None]
    received = [piece] + [across(piece, i) for i in (1, 2) if i < sections]
    for i in range(3, sections):
        received.append(across(after(piece, *received[1:3]), i))
    info = jnp.concatenate([expert_ids.T.astype(F32), probs.T], axis=0)[None]
    if square:
        sib0 = swap(piece, 1, 1)
        near0 = [swap(piece, 2, 4), swap(sib0, 2, 4)]
        info = after(info, near0[0])
        for bit in (2, 4, 1):
            info = jnp.concatenate([info, swap(info, bit, bit)], axis=0)
        place = owners ^ me
        place = place // 2 + place % 2 * 4
    else:
        info = lax.all_gather(info, "expert", axis=0, tiled=True)
        place = owners
    at = jnp.concatenate([jnp.stack([z, me * experts]), owners, place]).astype(jnp.int32)
    gated = lambda at: coefficients(at, info, topk, saved_gate, saved_up, slots // groups)
    if square:
        got = [after(x, info) for x in received[1:3]]
        near0 = [after(x, *got) for x in near0]
        pair1 = join(got, [swap(x, 1, 1) for x in got])
        first1 = swap(pair1, 2, 4)
        second0 = swap(near0[0], 4, 2)
        coefs = gated(after(at, pair1, *near0))
        got = [after(x, coefs[0]) for x in received[3:]]
        pair2 = join(got, [swap(x, 1, 1) for x in got])
        first1, second0 = after(first1, pair2), after(second0, pair2)
        second1 = swap(first1[:1], 4, 2)
        first2 = swap(after(pair2, first1), 2, 4)
        lot0 = [piece, sib0, *near0, *[swap(x, 1, 1) for x in near0]], [second0, swap(second0, 1, 1)]
        lot1 = [pair1, first1, swap(first1, 1, 1)]
        (most,) = hidden(at, [(None, [(0, lot0[0]), (1, lot1)])], tokens, after(w_down, coefs[0]))
        second1, first2, _ = lax.optimization_barrier((second1, first2, most))
        second2 = swap(first2[:1], 4, 2)
        lot1 = [second1, swap(second1, 1, 1)]
        (few,) = hidden(at, [(None, [(0, lot0[1]), (1, lot1)])], tokens, w_down)
        second2 = after(second2, few)
        lot2 = [pair2, first2, swap(first2, 1, 1)], [second2, swap(second2, 1, 1)]
        parts = [(most, [(3, lot2[0])]), (few, [(3, lot2[1])])]
    else:
        coefs = gated(at)
        gather = lambda xs: [lax.all_gather(jnp.concatenate(xs, axis=1), "expert", axis=0, tiled=True)]
        (h,) = hidden(at, [(None, [(0, gather(received[:3]))])], tokens, w_down)
        parts = [(h, [(3, gather(received[3:]))])]
    more = -(-2 * groups * experts * tokens // (16 * span)) * 16
    ag, au, info = hidden(at, parts, tokens, w_down, coefs, experts, moves, more)

    lots = ((3, sections), (2, 3), (1, 2), (0, 1))
    half = groups // 2
    last = [info]
    theirs, kept, sent, parts, routers = {}, {}, {}, {}, {}

    def run_expand(n, part, counts, other=None):
        a, b = lots[n]
        outs = expand(
            at, a, b - a, part, after(ag, *last), au, w_gate, w_up, sections, tokens, counts,
            info if n == 0 else None, other,
        )
        last[0] = outs[0]
        return outs

    def theirs_step(n):
        theirs[n] = swap(run_expand(n, 1, (half,))[0], 1, 1)

    def mine_step(n):
        alone, two, one = run_expand(n, 0, (1, 2, 1), theirs[n])
        kept[n] = alone, two, swap(one, 4, 2)

    def sent_step(n):
        _, two, one = kept[n]
        last[0] = pass_on(two, after(one, *last))
        sent[n] = swap(last[0], 2, 4)

    def hand_out(n, sums):
        a = lots[n][0]
        for k, x in enumerate(sums):
            if a + k == 0:
                parts[0] = x
                continue
            if n == 0 and k == 0:
                routers[0] = x[tokens:]
            x = across(x, a + k)
            parts[a + k] = x[:tokens]
            if n == 0:
                routers[a + k] = x[tokens:]
        if n == 0:
            routers.update({i: across(routers[0], i) for i in range(1, 3) if i < sections})

    def receive_step(n):
        got = after(sent[n], *last)
        sent[n] = got[:1], swap(got[1:], 1, 1)

    def final_step(n):
        last[0] = finish(after(kept[n][0], *last), *sent[n])
        hand_out(n, list(last[0]))

    if square:
        for step, n in (
            (theirs_step, 0),
            (theirs_step, 1),
            (mine_step, 0),
            (mine_step, 1),
            (sent_step, 0),
            (theirs_step, 2),
            (theirs_step, 3),
            (sent_step, 1),
            (mine_step, 2),
            (mine_step, 3),
            (receive_step, 0),
            (sent_step, 2),
            (final_step, 0),
            (receive_step, 1),
            (final_step, 1),
            (receive_step, 2),
            (sent_step, 3),
            (receive_step, 3),
            (final_step, 2),
            (final_step, 3),
        ):
            step(n)
    else:
        for n, (a, b) in enumerate(lots):
            outs = run_expand(n, 0, (groups,))
            sums = lax.psum_scatter(outs[0], "expert", scatter_dimension=0, tiled=True)[0]
            hand_out(n, list(sums))
    grad_in = add(*parts.values())

    router = functools.reduce(lambda a, b: a + b, [r.astype(F32) for r in routers.values()])
    count = groups * experts
    router = jnp.sum(router.reshape(-1)[: 2 * count * tokens].reshape(2, count, tokens), axis=0)
    match = expert_ids[None] == jnp.arange(count)[:, None, None]
    grad_probs = jnp.sum(jnp.where(match, router[:, :, None], 0.0), axis=0).astype(BF16)
    return (grad_in, grad_probs)


def solution(mesh):
    placed = (
        P("expert", "section"),
        P("expert", None),
        P("expert", None),
        P("expert", "section", None),
        P("expert", "section", None),
        P("expert", "section", None),
        P("expert", "section", None),
        P("expert", "section", None),
    )
    return jax.shard_map(
        local,
        mesh=mesh,
        in_specs=placed,
        out_specs=(P("expert", "section"), P("expert", None)),
        check_vma=False,
    )
```

```python
import functools

import jax
import jax.numpy as jnp
from jax import lax
from jax.experimental import pallas as pl
from jax.experimental.pallas import tpu as pltpu
from jax.sharding import PartitionSpec as P

F32, BF16 = jnp.float32, jnp.bfloat16
ROWS_BY_ROWS = (((1,), (1,)), ((), ()))
BASE = 10 << 20
WEIGHT = 16


def call(kernel, name, grid, in_specs, out_specs, out_shape, operands, flops, limit, scratch=()):
    outs = out_shape if isinstance(out_shape, list) else [out_shape]
    moved = sum(x.size * x.dtype.itemsize for x in [*operands, *outs])
    return pl.pallas_call(
        kernel,
        grid_spec=pltpu.PrefetchScalarGridSpec(
            num_scalar_prefetch=1,
            grid=grid,
            in_specs=in_specs,
            out_specs=out_specs,
            scratch_shapes=scratch,
        ),
        out_shape=out_shape,
        compiler_params=pltpu.CompilerParams(vmem_limit_bytes=min(limit, 56 << 20)),
        cost_estimate=pl.CostEstimate(flops=WEIGHT * flops, bytes_accessed=moved, transcendentals=0),
        name=name,
    )(*operands)


def coefficient_kernel(capacity, topk, at_ref, info_ref, gate_ref, up_ref, cg_ref, cu_ref, cr_ref, columns_ref):
    experts, width, slots = gate_ref.shape
    blocks, _, tokens = info_ref.shape

    @pl.when(pl.program_id(0) == 0)
    def _():
        before = lax.broadcasted_iota(jnp.int32, (tokens, tokens), 0)
        earlier = (before < lax.broadcasted_iota(jnp.int32, (tokens, tokens), 1)).astype(BF16)
        for b in range(blocks):
            info = info_ref[at_ref[2 + blocks + b]]
            ids, prob = info[:topk], info[topk:]
            named, weight = [], []
            for e in range(experts):
                chosen = ids == (at_ref[1] + e).astype(F32)
                named.append(jnp.max(jnp.where(chosen, 1.0, 0.0), axis=0, keepdims=True))
                weight.append(jnp.sum(jnp.where(chosen, prob, 0.0), axis=0, keepdims=True))
            named = jnp.concatenate(named, axis=0)
            position = jnp.dot(named.astype(BF16), earlier, preferred_element_type=F32)
            slot = jnp.where(named > 0.0, position + (at_ref[2 + b] * capacity).astype(F32), -1.0)
            fill = jnp.zeros((8 - 2 * experts, tokens), F32)
            columns_ref[b * tokens : (b + 1) * tokens] = jnp.transpose(
                jnp.concatenate([slot, *weight, fill], axis=0)
            )

    rows = cg_ref.shape[0]
    columns = columns_ref[pl.ds(pl.multiple_of(pl.program_id(0) * rows, rows), rows)]
    number = lax.broadcasted_iota(jnp.int32, (rows, slots), 1).astype(F32)
    for e in range(experts):
        pick = jnp.where(columns[:, e : e + 1] == number, 1.0, 0.0).astype(BF16)
        g = lax.dot_general(pick, gate_ref[e], ROWS_BY_ROWS, preferred_element_type=F32)
        u = lax.dot_general(pick, up_ref[e], ROWS_BY_ROWS, preferred_element_type=F32)
        p = columns[:, experts + e : experts + e + 1]
        sg = 1.0 / (1.0 + jnp.exp(-g))
        silu = g * sg
        span = slice(e * width, (e + 1) * width)
        cg_ref[:, span] = (u * sg * (1.0 + g * (1.0 - sg)) * p).astype(BF16)
        cu_ref[:, span] = (silu * p).astype(BF16)
        cr_ref[:, span] = (silu * u).astype(BF16)


def coefficients(at, info, topk, saved_gate, saved_up, capacity):
    experts, width, slots = saved_gate.shape
    blocks, _, tokens = info.shape
    tile = (4 if blocks % 4 == 0 else 1) * tokens
    total = blocks * tokens
    whole = lambda x: pl.BlockSpec(x.shape, lambda i, at: (0, 0, 0))
    out = pl.BlockSpec((tile, experts * width), lambda i, at: (i, 0))
    return call(
        functools.partial(coefficient_kernel, capacity, topk),
        "coefficients",
        (total // tile,),
        [whole(info), whole(saved_gate), whole(saved_up)],
        [out] * 3,
        [jax.ShapeDtypeStruct((total, experts * width), BF16)] * 3,
        (at, info, saved_gate, saved_up),
        4 * total * slots * experts * width,
        2 * BASE,
        [pltpu.VMEM((total, 8), F32)],
    )


def products(plan, refs):
    sums = []
    for before, lots in plan:
        total = None if before is None else refs[before][...]
        for blocks, weights in lots:
            for k, weight in enumerate(weights):
                xs = [refs[i][:, k] for i in blocks]
                xs = [x.reshape(x.shape[0] * x.shape[1], x.shape[2]) for x in xs]
                x = xs[0] if len(xs) == 1 else jnp.concatenate(xs, axis=0)
                y = lax.dot_general(x, refs[weight][...], ROWS_BY_ROWS, preferred_element_type=F32)
                total = y if total is None else total + y
        sums.append(total)
    return sums


def early_kernel(plan, at_ref, *refs):
    for out_ref, h in zip(refs[len(refs) - len(plan) :], products(plan, refs)):
        out_ref[...] = h


def late_kernel(plan, experts, width, moves, at_ref, *refs):
    cg_ref, cu_ref, cr_ref, ag_ref, au_ref, info_ref, r_ref = refs[len(refs) - 7 :]
    total, tile = ag_ref.shape
    tokens = total // len(moves)

    @pl.when(pl.program_id(0) == 0)
    def _():
        r_ref[...] = jnp.zeros_like(r_ref)

    at = 0
    for h in products(plan, refs):
        rows = slice(at, at + h.shape[0])
        ag = (h * cg_ref[rows].astype(F32)).astype(BF16)
        au = (h * cu_ref[rows].astype(F32)).astype(BF16)
        terms = h * cr_ref[rows].astype(F32)
        for i in range(h.shape[0] // tokens):
            j = moves[at // tokens + i]
            to, of = slice(j * tokens, (j + 1) * tokens), slice(i * tokens, (i + 1) * tokens)
            ag_ref[to], au_ref[to] = ag[of], au[of]
        unit = pl.program_id(0) * tile + lax.broadcasted_iota(jnp.int32, terms.shape, 1)
        for e in range(experts):
            own = (unit >= e * width) & (unit < (e + 1) * width)
            r_ref[rows, e : e + 1] += jnp.sum(jnp.where(own, terms, 0.0), axis=1, keepdims=True)
        at += h.shape[0]

    @pl.when(pl.program_id(0) == pl.num_programs(0) - 1)
    def _():
        more, span = info_ref.shape[1:]
        per, count = span // tokens, experts * len(moves)
        for i, j in enumerate(moves):
            value = jnp.transpose(r_ref[i * tokens : (i + 1) * tokens])
            high = value.astype(BF16).astype(F32)
            parts = []
            for x in (high, value - high):
                for n in range(count):
                    own = [jnp.where(at_ref[1] + e == n, x[e : e + 1], 0.0) for e in range(experts)]
                    parts.append(functools.reduce(lambda p, q: p + q, own))
            parts += [jnp.zeros((1, tokens), F32)] * (more * per - len(parts))
            lines = [jnp.concatenate(parts[n : n + per], axis=1) for n in range(0, more * per, per)]
            info_ref[j] = jnp.concatenate(lines, axis=0).astype(BF16)


def tile_of(n):
    return 256 if n % 256 == 0 else 128 if n % 128 == 0 else n


def hidden(at, parts, tokens, w_down, coefs=None, experts=None, moves=None, more=None):
    units = w_down.shape[0]
    tile = tile_of(units)
    specs, operands, weights, plan, sizes, work, held = [], [], {}, [], [], 0, 0

    def operand(x, spec):
        operands.append(x)
        specs.append(spec)
        return len(operands) - 1

    for before, lots in parts:
        size = tokens * sum(b.shape[0] for b in lots[0][1])
        of = None
        if before is not None:
            of = operand(before, pl.BlockSpec((size, tile), lambda n, at: (0, n)))
        steps = []
        for first, blocks in lots:
            pieces, span = blocks[0].shape[1], blocks[0].shape[3]
            whole = lambda b: pl.BlockSpec((b.shape[0], pieces, tokens, span), lambda n, at: (0, 0, 0, 0))
            rows = [operand(b, whole(b)) for b in blocks]
            for i in range(first, first + pieces):
                if i not in weights:
                    weights[i] = operand(w_down, pl.BlockSpec((tile, span), lambda n, at, i=i: (n, at[0] ^ i)))
            steps.append((rows, [weights[i] for i in range(first, first + pieces)]))
            work += size * units * pieces * span
            held += 4 * size * pieces * span
        plan.append((of, steps))
        sizes.append(size)
    total = sum(sizes)
    limit = BASE + held + 16 * total * tile
    grid = (units // tile,)
    column = lambda n: pl.BlockSpec((n, tile), lambda n, at: (0, n))
    if coefs is None:
        out = [jax.ShapeDtypeStruct((n, units), F32) for n in sizes]
        kernel = functools.partial(early_kernel, plan)
        return call(
            kernel, "hidden_early", grid, specs, [column(n) for n in sizes], out, [at, *operands], work, limit
        )
    kernel = functools.partial(late_kernel, plan, experts, units // experts, moves)
    outs = [column(total), column(total), pl.BlockSpec((len(moves), more, span), lambda n, at: (0, 0, 0))]
    shapes = [jax.ShapeDtypeStruct((total, units), BF16)] * 2
    shapes.append(jax.ShapeDtypeStruct((len(moves), more, span), BF16))
    return call(
        kernel,
        "hidden_late",
        grid,
        specs + [column(total)] * 3,
        outs,
        shapes,
        [at, *operands, *coefs],
        work,
        limit,
        [pltpu.VMEM((total, 8), F32)],
    )


def expand_kernel(counts, adds, carries, at_ref, ag_ref, au_ref, wg_ref, wu_ref, *refs):
    other, refs = refs[: int(adds)], refs[int(adds) :]
    info, outs = refs[: int(carries)], refs[int(carries) :]
    width = outs[0].shape[3]
    rows = ag_ref.shape[0] // sum(counts)
    tile = tile_of(width)
    for at in range(0, width, tile):
        span = slice(at, at + tile)
        y = jnp.dot(ag_ref[...], wg_ref[:, span], preferred_element_type=F32)
        y = y + jnp.dot(au_ref[...], wu_ref[:, span], preferred_element_type=F32)
        i = 0
        for out, count in zip(outs, counts):
            for j in range(count):
                part = y[i * rows : (i + 1) * rows]
                if adds:
                    part = part + other[0][i, 0, :rows, span].astype(F32)
                out[j, 0, :rows, span] = part.astype(BF16)
                if carries:
                    part = info[0][i, :, span]
                    if adds:
                        part = (part.astype(F32) + other[0][i, 0, rows:, span].astype(F32)).astype(BF16)
                    out[j, 0, rows:, span] = part
                i += 1


def expand(at, first, pieces, part, ag, au, w_gate, w_up, sections, rows, counts, info=None, other=None):
    units = ag.shape[1]
    number = sum(counts)
    span = w_gate.shape[1] // sections
    half = max(span // 2, 128)
    per = span // half
    more = 0 if info is None else info.shape[1]
    some = pl.BlockSpec((number * rows, units), lambda k, j, at: (part, 0))
    weight = pl.BlockSpec((units, half), lambda k, j, at: (0, (at[0] ^ (first + k)) * per + j))
    block = lambda n: pl.BlockSpec((n, 1, rows + more, half), lambda k, j, at: (0, k, 0, j))
    specs, operands = [some, some, weight, weight], [at, ag, au, w_gate, w_up]
    if other is not None:
        specs, operands = specs + [block(number)], operands + [other]
    if info is not None:
        specs.append(pl.BlockSpec((number, more, half), lambda k, j, at: (part, 0, j)))
        operands.append(info)
    return call(
        functools.partial(expand_kernel, counts, other is not None, info is not None),
        "expand",
        (pieces, per),
        specs,
        [block(n) for n in counts],
        [jax.ShapeDtypeStruct((n, pieces, rows + more, span), BF16) for n in counts],
        operands,
        2 * number * rows * units * pieces * span,
        BASE + 8 * number * rows * units + 4 * number * rows * half,
    )


def small(kernel, name, out_shape, operands, specs=None, scratch=(), out_spec=None, flops=1 << 30):
    specs = [pl.BlockSpec(memory_space=pltpu.VMEM)] * len(operands) if specs is None else specs
    return pl.pallas_call(
        kernel,
        in_specs=specs,
        out_specs=pl.BlockSpec(memory_space=pltpu.VMEM) if out_spec is None else out_spec,
        out_shape=out_shape,
        scratch_shapes=scratch,
        compiler_params=pltpu.CompilerParams(vmem_limit_bytes=BASE),
        cost_estimate=pl.CostEstimate(flops=flops, bytes_accessed=0, transcendentals=0),
        name=name,
    )(*operands)


def join_kernel(counts, *refs):
    xs, out, sems = refs[: sum(counts)], refs[-2], refs[-1]
    copies, n = [], 0
    for i, count in enumerate(counts):
        for k in range(count):
            copies.append(pltpu.make_async_copy(xs[n].at[0, 0], out.at[i, k], sems.at[n]))
            n += 1
    for c in copies:
        c.start()
    for c in copies:
        c.wait()


def join(*rows):
    counts = [len(r) for r in rows]
    xs = [x for r in rows for x in r]
    somewhere = pl.BlockSpec(memory_space=pl.ANY)
    return small(
        functools.partial(join_kernel, counts),
        "join",
        jax.ShapeDtypeStruct((len(rows), counts[0], *xs[0].shape[2:]), xs[0].dtype),
        xs,
        specs=[somewhere] * len(xs),
        scratch=[pltpu.SemaphoreType.DMA((len(xs),))],
        out_spec=somewhere,
        flops=0,
    )


def pass_on_kernel(two_ref, one_ref, out_ref):
    out_ref[0] = (two_ref[0].astype(F32) + one_ref[0].astype(F32)).astype(BF16)
    out_ref[1] = two_ref[1]


def pass_on(two, one):
    return small(pass_on_kernel, "pass_on", jax.ShapeDtypeStruct(two.shape, BF16), (two, one), flops=1 << 32)


def finish_kernel(rows, a_ref, b_ref, c_ref, *refs):
    extra, out_ref = refs[:-1], refs[-1]
    y = a_ref[0, 0].astype(F32) + b_ref[0, 0].astype(F32) + c_ref[0, 0].astype(F32)
    if extra:
        got_ref, own_ref = extra
        out_ref[:rows] = (y + got_ref[:rows].astype(F32)).astype(BF16)
        more = got_ref[rows:].astype(F32) + own_ref[rows:].astype(F32)
        out_ref[rows:] = more.astype(BF16)
    else:
        out_ref[...] = y.astype(BF16)


def finish(rows, a, b, c, *extra):
    shape = extra[0].shape if extra else a.shape[2:]
    kernel = functools.partial(finish_kernel, rows)
    return small(kernel, "finish", jax.ShapeDtypeStruct(shape, BF16), (a, b, c, *extra), flops=1 << 30)


def add(*terms):
    return functools.reduce(lambda a, b: a + b, [t.astype(F32) for t in terms]).astype(BF16)


def after(x, *others):
    return lax.optimization_barrier((x, *others))[0]


def local(grad_out, probs, expert_ids, w_gate, w_up, w_down, saved_gate, saved_up):
    groups, sections = lax.axis_size("expert"), lax.axis_size("section")
    me, z = lax.axis_index("expert"), lax.axis_index("section")
    experts, units, features = w_gate.shape
    slots = saved_gate.shape[2]
    tokens, topk = expert_ids.shape
    span = grad_out.shape[1]
    square = groups == 8 and sections == 4
    flat = lambda w: w.reshape(experts * units, features)
    w_gate, w_up, w_down = flat(w_gate), flat(w_up), flat(w_down)
    core = me % 2
    near = jnp.where(core == 0, 2, 4)
    far = 6 - near

    def swap(x, even, odd):
        return lax.ppermute(x, "expert", [(i, i ^ (even, odd)[i % 2]) for i in range(groups)])

    def across(x, by):
        return lax.ppermute(x, "section", [(i, i ^ by) for i in range(sections)])

    if square:
        owners = jnp.stack([me, me ^ 1, me ^ near, me ^ near ^ 1, me ^ 1 ^ far, me ^ far, me ^ 6, me ^ 7])
        moves = (0, 4, 1, 2, 5, 6, 3, 7)
    else:
        owners, moves = jnp.arange(groups), tuple(range(groups))

    piece = grad_out[None, None]
    received = [piece] + [across(piece, i) for i in (1, 2) if i < sections]
    for i in range(3, sections):
        received.append(across(after(piece, *received[1:3]), i))
    info = jnp.concatenate([expert_ids.T.astype(F32), probs.T], axis=0)[None]
    if square:
        sib0 = swap(piece, 1, 1)
        near0 = [swap(piece, 2, 4), swap(sib0, 2, 4)]
        info = after(info, near0[0])
        for bit in (2, 4, 1):
            info = jnp.concatenate([info, swap(info, bit, bit)], axis=0)
        place = owners ^ me
        place = place // 2 + place % 2 * 4
    else:
        info = lax.all_gather(info, "expert", axis=0, tiled=True)
        place = owners
    at = jnp.concatenate([jnp.stack([z, me * experts]), owners, place]).astype(jnp.int32)
    gated = lambda at: coefficients(at, info, topk, saved_gate, saved_up, slots // groups)
    if square:
        got = [after(x, info) for x in received[1:3]]
        near0 = [after(x, *got) for x in near0]
        pair1 = join(got, [swap(x, 1, 1) for x in got])
        first1 = swap(pair1, 2, 4)
        second0 = swap(near0[0], 4, 2)
        coefs = gated(after(at, pair1, *near0))
        got = [after(x, coefs[0]) for x in received[3:]]
        pair2 = join(got, [swap(x, 1, 1) for x in got])
        first1, second0 = after(first1, pair2), after(second0, pair2)
        second1 = swap(first1[:1], 4, 2)
        first2 = swap(after(pair2, first1), 2, 4)
        lot0 = [piece, sib0, *near0, *[swap(x, 1, 1) for x in near0]], [second0, swap(second0, 1, 1)]
        lot1 = [pair1, first1, swap(first1, 1, 1)]
        (most,) = hidden(at, [(None, [(0, lot0[0]), (1, lot1)])], tokens, after(w_down, coefs[0]))
        second1, first2, _ = lax.optimization_barrier((second1, first2, most))
        second2 = swap(first2[:1], 4, 2)
        lot1 = [second1, swap(second1, 1, 1)]
        (few,) = hidden(at, [(None, [(0, lot0[1]), (1, lot1)])], tokens, w_down)
        second2 = after(second2, few)
        lot2 = [pair2, first2, swap(first2, 1, 1)], [second2, swap(second2, 1, 1)]
        parts = [(most, [(3, lot2[0])]), (few, [(3, lot2[1])])]
    else:
        coefs = gated(at)
        gather = lambda xs: [lax.all_gather(jnp.concatenate(xs, axis=1), "expert", axis=0, tiled=True)]
        (h,) = hidden(at, [(None, [(0, gather(received[:3]))])], tokens, w_down)
        parts = [(h, [(3, gather(received[3:]))])]
    more = -(-2 * groups * experts * tokens // (16 * span)) * 16
    ag, au, info = hidden(at, parts, tokens, w_down, coefs, experts, moves, more)

    lots = ((3, sections), (2, 3), (1, 2), (0, 1))
    half = groups // 2
    last = [info]
    theirs, kept, sent, parts, firsts = {}, {}, {}, {}, {}

    def run_expand(n, part, counts, other=None):
        a, b = lots[n]
        outs = expand(
            at, a, b - a, part, after(ag, *last), au, w_gate, w_up, sections, tokens, counts,
            info if n == 0 else None, other,
        )
        last[0] = outs[0]
        return outs

    def theirs_step(n):
        theirs[n] = swap(run_expand(n, 1, (half,))[0], 1, 1)

    def mine_step(n):
        alone, two, one = run_expand(n, 0, (1, 2, 1), theirs[n])
        kept[n] = alone, two, swap(one, 4, 2)

    def sent_step(n):
        _, two, one = kept[n]
        last[0] = pass_on(two, after(one, *last))
        sent[n] = swap(last[0], 2, 4)

    def receive_step(n):
        got = after(sent[n], *last)
        sent[n] = got[:1], swap(got[1:], 1, 1)

    def final_step(n):
        extra = (parts[0], firsts[0]) if n == 1 else ()
        x = finish(tokens, after(kept[n][0], *last), *sent[n], *extra)
        last[0] = firsts[n] = x
        parts[n] = across(x, (1, 2, 1)[n]) if n < 3 else x

    if square:
        for step, n in (
            (theirs_step, 0),
            (theirs_step, 1),
            (mine_step, 0),
            (mine_step, 1),
            (sent_step, 0),
            (theirs_step, 2),
            (theirs_step, 3),
            (sent_step, 1),
            (receive_step, 0),
            (mine_step, 2),
            (mine_step, 3),
            (sent_step, 2),
            (final_step, 0),
            (receive_step, 1),
            (sent_step, 3),
            (final_step, 1),
            (receive_step, 2),
            (final_step, 2),
            (receive_step, 3),
            (final_step, 3),
        ):
            step(n)
        parts[1] = after(parts[1], firsts[2])
        grad_in = add(parts[1][:tokens], parts[2], parts[3])
        router = firsts[1][tokens:].astype(F32) + parts[1][tokens:].astype(F32)
    else:
        terms = []
        for n, (a, b) in enumerate(lots):
            sums = lax.psum_scatter(run_expand(n, 0, (groups,))[0], "expert", scatter_dimension=0, tiled=True)[0]
            if n == 0:
                router = lax.psum(sums[0, tokens:].astype(F32), "section")
            terms += [across(sums[i - a, :tokens], i) if i else sums[0] for i in range(a, b)]
        grad_in = add(*terms)

    count = groups * experts
    router = jnp.sum(router.reshape(-1)[: 2 * count * tokens].reshape(2, count, tokens), axis=0)
    match = expert_ids[None] == jnp.arange(count)[:, None, None]
    grad_probs = jnp.sum(jnp.where(match, router[:, :, None], 0.0), axis=0).astype(BF16)
    return (grad_in, grad_probs)


def solution(mesh):
    placed = (
        P("expert", "section"),
        P("expert", None),
        P("expert", None),
        P("expert", "section", None),
        P("expert", "section", None),
        P("expert", "section", None),
        P("expert", "section", None),
        P("expert", "section", None),
    )
    return jax.shard_map(
        local,
        mesh=mesh,
        in_specs=placed,
        out_specs=(P("expert", "section"), P("expert", None)),
        check_vma=False,
    )
```

```python
import functools

import jax
import jax.numpy as jnp
from jax import lax
from jax.experimental import pallas as pl
from jax.experimental.pallas import tpu as pltpu
from jax.sharding import PartitionSpec as P

F32, BF16 = jnp.float32, jnp.bfloat16
ROWS_BY_ROWS = (((1,), (1,)), ((), ()))
BASE = 10 << 20
WEIGHT = 16


def call(kernel, name, grid, in_specs, out_specs, out_shape, operands, flops, limit, scratch=()):
    outs = out_shape if isinstance(out_shape, list) else [out_shape]
    moved = sum(x.size * x.dtype.itemsize for x in [*operands, *outs])
    return pl.pallas_call(
        kernel,
        grid_spec=pltpu.PrefetchScalarGridSpec(
            num_scalar_prefetch=1,
            grid=grid,
            in_specs=in_specs,
            out_specs=out_specs,
            scratch_shapes=scratch,
        ),
        out_shape=out_shape,
        compiler_params=pltpu.CompilerParams(vmem_limit_bytes=min(limit, 56 << 20)),
        cost_estimate=pl.CostEstimate(flops=WEIGHT * flops, bytes_accessed=moved, transcendentals=0),
        name=name,
    )(*operands)


def coefficient_kernel(capacity, topk, at_ref, info_ref, gate_ref, up_ref, cg_ref, cu_ref, cr_ref, columns_ref):
    experts, width, slots = gate_ref.shape
    blocks, _, tokens = info_ref.shape

    @pl.when(pl.program_id(0) == 0)
    def _():
        before = lax.broadcasted_iota(jnp.int32, (tokens, tokens), 0)
        earlier = (before < lax.broadcasted_iota(jnp.int32, (tokens, tokens), 1)).astype(BF16)
        for b in range(blocks):
            info = info_ref[at_ref[2 + blocks + b]]
            ids, prob = info[:topk], info[topk:]
            named, weight = [], []
            for e in range(experts):
                chosen = ids == (at_ref[1] + e).astype(F32)
                named.append(jnp.max(jnp.where(chosen, 1.0, 0.0), axis=0, keepdims=True))
                weight.append(jnp.sum(jnp.where(chosen, prob, 0.0), axis=0, keepdims=True))
            named = jnp.concatenate(named, axis=0)
            position = jnp.dot(named.astype(BF16), earlier, preferred_element_type=F32)
            slot = jnp.where(named > 0.0, position + (at_ref[2 + b] * capacity).astype(F32), -1.0)
            fill = jnp.zeros((8 - 2 * experts, tokens), F32)
            columns_ref[b * tokens : (b + 1) * tokens] = jnp.transpose(
                jnp.concatenate([slot, *weight, fill], axis=0)
            )

    rows = cg_ref.shape[0]
    columns = columns_ref[pl.ds(pl.multiple_of(pl.program_id(0) * rows, rows), rows)]
    number = lax.broadcasted_iota(jnp.int32, (rows, slots), 1).astype(F32)
    for e in range(experts):
        pick = jnp.where(columns[:, e : e + 1] == number, 1.0, 0.0).astype(BF16)
        g = lax.dot_general(pick, gate_ref[e], ROWS_BY_ROWS, preferred_element_type=F32)
        u = lax.dot_general(pick, up_ref[e], ROWS_BY_ROWS, preferred_element_type=F32)
        p = columns[:, experts + e : experts + e + 1]
        sg = 1.0 / (1.0 + jnp.exp(-g))
        silu = g * sg
        span = slice(e * width, (e + 1) * width)
        cg_ref[:, span] = (u * sg * (1.0 + g * (1.0 - sg)) * p).astype(BF16)
        cu_ref[:, span] = (silu * p).astype(BF16)
        cr_ref[:, span] = (silu * u).astype(BF16)


def coefficients(at, info, topk, saved_gate, saved_up, capacity):
    experts, width, slots = saved_gate.shape
    blocks, _, tokens = info.shape
    tile = (4 if blocks % 4 == 0 else 1) * tokens
    total = blocks * tokens
    whole = lambda x: pl.BlockSpec(x.shape, lambda i, at: (0, 0, 0))
    out = pl.BlockSpec((tile, experts * width), lambda i, at: (i, 0))
    return call(
        functools.partial(coefficient_kernel, capacity, topk),
        "coefficients",
        (total // tile,),
        [whole(info), whole(saved_gate), whole(saved_up)],
        [out] * 3,
        [jax.ShapeDtypeStruct((total, experts * width), BF16)] * 3,
        (at, info, saved_gate, saved_up),
        4 * total * slots * experts * width,
        2 * BASE,
        [pltpu.VMEM((total, 8), F32)],
    )


def products(plan, refs):
    sums = []
    for before, lots in plan:
        total = None if before is None else refs[before][...]
        for blocks, weights in lots:
            for k, weight in enumerate(weights):
                xs = [refs[i][:, k] for i in blocks]
                xs = [x.reshape(x.shape[0] * x.shape[1], x.shape[2]) for x in xs]
                x = xs[0] if len(xs) == 1 else jnp.concatenate(xs, axis=0)
                y = lax.dot_general(x, refs[weight][...], ROWS_BY_ROWS, preferred_element_type=F32)
                total = y if total is None else total + y
        sums.append(total)
    return sums


def early_kernel(plan, at_ref, *refs):
    for out_ref, h in zip(refs[len(refs) - len(plan) :], products(plan, refs)):
        out_ref[...] = h


def late_kernel(plan, experts, width, moves, at_ref, *refs):
    cg_ref, cu_ref, cr_ref, ag_ref, au_ref, info_ref, r_ref = refs[len(refs) - 7 :]
    total, tile = ag_ref.shape
    tokens = total // len(moves)

    @pl.when(pl.program_id(0) == 0)
    def _():
        r_ref[...] = jnp.zeros_like(r_ref)

    at = 0
    for h in products(plan, refs):
        rows = slice(at, at + h.shape[0])
        ag = (h * cg_ref[rows].astype(F32)).astype(BF16)
        au = (h * cu_ref[rows].astype(F32)).astype(BF16)
        terms = h * cr_ref[rows].astype(F32)
        for i in range(h.shape[0] // tokens):
            j = moves[at // tokens + i]
            to, of = slice(j * tokens, (j + 1) * tokens), slice(i * tokens, (i + 1) * tokens)
            ag_ref[to], au_ref[to] = ag[of], au[of]
        unit = pl.program_id(0) * tile + lax.broadcasted_iota(jnp.int32, terms.shape, 1)
        for e in range(experts):
            own = (unit >= e * width) & (unit < (e + 1) * width)
            r_ref[rows, e : e + 1] += jnp.sum(jnp.where(own, terms, 0.0), axis=1, keepdims=True)
        at += h.shape[0]

    @pl.when(pl.program_id(0) == pl.num_programs(0) - 1)
    def _():
        more, span = info_ref.shape[1:]
        per, count = span // tokens, experts * len(moves)
        for i, j in enumerate(moves):
            value = jnp.transpose(r_ref[i * tokens : (i + 1) * tokens])
            high = value.astype(BF16).astype(F32)
            parts = []
            for x in (high, value - high):
                for n in range(count):
                    own = [jnp.where(at_ref[1] + e == n, x[e : e + 1], 0.0) for e in range(experts)]
                    parts.append(functools.reduce(lambda p, q: p + q, own))
            parts += [jnp.zeros((1, tokens), F32)] * (more * per - len(parts))
            lines = [jnp.concatenate(parts[n : n + per], axis=1) for n in range(0, more * per, per)]
            info_ref[j] = jnp.concatenate(lines, axis=0).astype(BF16)


def tile_of(n):
    return 256 if n % 256 == 0 else 128 if n % 128 == 0 else n


def hidden(at, parts, tokens, w_down, coefs=None, experts=None, moves=None, more=None):
    units = w_down.shape[0]
    tile = tile_of(units)
    specs, operands, weights, plan, sizes, work, held = [], [], {}, [], [], 0, 0

    def operand(x, spec):
        operands.append(x)
        specs.append(spec)
        return len(operands) - 1

    for before, lots in parts:
        size = tokens * sum(b.shape[0] for b in lots[0][1])
        of = None
        if before is not None:
            of = operand(before, pl.BlockSpec((size, tile), lambda n, at: (0, n)))
        steps = []
        for first, blocks in lots:
            pieces, span = blocks[0].shape[1], blocks[0].shape[3]
            whole = lambda b: pl.BlockSpec((b.shape[0], pieces, tokens, span), lambda n, at: (0, 0, 0, 0))
            rows = [operand(b, whole(b)) for b in blocks]
            for i in range(first, first + pieces):
                if i not in weights:
                    weights[i] = operand(w_down, pl.BlockSpec((tile, span), lambda n, at, i=i: (n, at[0] ^ i)))
            steps.append((rows, [weights[i] for i in range(first, first + pieces)]))
            work += size * units * pieces * span
            held += 4 * size * pieces * span
        plan.append((of, steps))
        sizes.append(size)
    total = sum(sizes)
    limit = BASE + held + 16 * total * tile
    grid = (units // tile,)
    column = lambda n: pl.BlockSpec((n, tile), lambda n, at: (0, n))
    if coefs is None:
        out = [jax.ShapeDtypeStruct((n, units), F32) for n in sizes]
        kernel = functools.partial(early_kernel, plan)
        return call(
            kernel, "hidden_early", grid, specs, [column(n) for n in sizes], out, [at, *operands], work, limit
        )
    kernel = functools.partial(late_kernel, plan, experts, units // experts, moves)
    outs = [column(total), column(total), pl.BlockSpec((len(moves), more, span), lambda n, at: (0, 0, 0))]
    shapes = [jax.ShapeDtypeStruct((total, units), BF16)] * 2
    shapes.append(jax.ShapeDtypeStruct((len(moves), more, span), BF16))
    return call(
        kernel,
        "hidden_late",
        grid,
        specs + [column(total)] * 3,
        outs,
        shapes,
        [at, *operands, *coefs],
        work,
        limit,
        [pltpu.VMEM((total, 8), F32)],
    )


def expand_kernel(counts, adds, carries, at_ref, ag_ref, au_ref, wg_ref, wu_ref, *refs):
    other, refs = refs[: int(adds)], refs[int(adds) :]
    info, outs = refs[: int(carries)], refs[int(carries) :]
    width = outs[0].shape[3]
    rows = ag_ref.shape[0] // sum(counts)
    tile = tile_of(width)
    for at in range(0, width, tile):
        span = slice(at, at + tile)
        y = jnp.dot(ag_ref[...], wg_ref[:, span], preferred_element_type=F32)
        y = y + jnp.dot(au_ref[...], wu_ref[:, span], preferred_element_type=F32)
        i = 0
        for out, count in zip(outs, counts):
            for j in range(count):
                part = y[i * rows : (i + 1) * rows]
                if adds:
                    part = part + other[0][i, 0, :rows, span].astype(F32)
                out[j, 0, :rows, span] = part.astype(BF16)
                if carries:
                    part = info[0][i, :, span]
                    if adds:
                        part = (part.astype(F32) + other[0][i, 0, rows:, span].astype(F32)).astype(BF16)
                    out[j, 0, rows:, span] = part
                i += 1


def expand(at, first, pieces, part, ag, au, w_gate, w_up, sections, rows, counts, info=None, other=None):
    units = ag.shape[1]
    number = sum(counts)
    span = w_gate.shape[1] // sections
    half = max(span // 2, 128)
    per = span // half
    more = 0 if info is None else info.shape[1]
    some = pl.BlockSpec((number * rows, units), lambda k, j, at: (part, 0))
    weight = pl.BlockSpec((units, half), lambda k, j, at: (0, (at[0] ^ (first + k)) * per + j))
    block = lambda n: pl.BlockSpec((n, 1, rows + more, half), lambda k, j, at: (0, k, 0, j))
    specs, operands = [some, some, weight, weight], [at, ag, au, w_gate, w_up]
    if other is not None:
        specs, operands = specs + [block(number)], operands + [other]
    if info is not None:
        specs.append(pl.BlockSpec((number, more, half), lambda k, j, at: (part, 0, j)))
        operands.append(info)
    return call(
        functools.partial(expand_kernel, counts, other is not None, info is not None),
        "expand",
        (pieces, per),
        specs,
        [block(n) for n in counts],
        [jax.ShapeDtypeStruct((n, pieces, rows + more, span), BF16) for n in counts],
        operands,
        2 * number * rows * units * pieces * span,
        BASE + 8 * number * rows * units + 4 * number * rows * half,
    )


def small(kernel, name, out_shape, operands, specs=None, scratch=(), out_spec=None, flops=1 << 30):
    specs = [pl.BlockSpec(memory_space=pltpu.VMEM)] * len(operands) if specs is None else specs
    return pl.pallas_call(
        kernel,
        in_specs=specs,
        out_specs=pl.BlockSpec(memory_space=pltpu.VMEM) if out_spec is None else out_spec,
        out_shape=out_shape,
        scratch_shapes=scratch,
        compiler_params=pltpu.CompilerParams(vmem_limit_bytes=BASE),
        cost_estimate=pl.CostEstimate(flops=flops, bytes_accessed=0, transcendentals=0),
        name=name,
    )(*operands)


def join_kernel(counts, *refs):
    xs, out, sems = refs[: sum(counts)], refs[-2], refs[-1]
    copies, n = [], 0
    for i, count in enumerate(counts):
        for k in range(count):
            copies.append(pltpu.make_async_copy(xs[n].at[0, 0], out.at[i, k], sems.at[n]))
            n += 1
    for c in copies:
        c.start()
    for c in copies:
        c.wait()


def join(*rows):
    counts = [len(r) for r in rows]
    xs = [x for r in rows for x in r]
    somewhere = pl.BlockSpec(memory_space=pl.ANY)
    return small(
        functools.partial(join_kernel, counts),
        "join",
        jax.ShapeDtypeStruct((len(rows), counts[0], *xs[0].shape[2:]), xs[0].dtype),
        xs,
        specs=[somewhere] * len(xs),
        scratch=[pltpu.SemaphoreType.DMA((len(xs),))],
        out_spec=somewhere,
        flops=0,
    )


def pass_on_kernel(two_ref, one_ref, out_ref):
    out_ref[0] = (two_ref[0].astype(F32) + one_ref[0].astype(F32)).astype(BF16)
    out_ref[1] = two_ref[1]


def pass_on(two, one):
    return small(pass_on_kernel, "pass_on", jax.ShapeDtypeStruct(two.shape, BF16), (two, one), flops=1 << 32)


def finish_kernel(rows, a_ref, b_ref, c_ref, *refs):
    extra, out_ref = refs[:-1], refs[-1]
    y = a_ref[0, 0].astype(F32) + b_ref[0, 0].astype(F32) + c_ref[0, 0].astype(F32)
    if extra:
        got_ref, own_ref = extra
        out_ref[:rows] = (y + got_ref[:rows].astype(F32)).astype(BF16)
        more = got_ref[rows:].astype(F32) + own_ref[rows:].astype(F32)
        out_ref[rows:] = more.astype(BF16)
    else:
        out_ref[...] = y.astype(BF16)


def finish(rows, a, b, c, *extra):
    shape = extra[0].shape if extra else a.shape[2:]
    kernel = functools.partial(finish_kernel, rows)
    return small(kernel, "finish", jax.ShapeDtypeStruct(shape, BF16), (a, b, c, *extra), flops=1 << 30)


def add(*terms):
    return functools.reduce(lambda a, b: a + b, [t.astype(F32) for t in terms]).astype(BF16)


def after(x, *others):
    return lax.optimization_barrier((x, *others))[0]


def local(grad_out, probs, expert_ids, w_gate, w_up, w_down, saved_gate, saved_up):
    groups, sections = lax.axis_size("expert"), lax.axis_size("section")
    me, z = lax.axis_index("expert"), lax.axis_index("section")
    experts, units, features = w_gate.shape
    slots = saved_gate.shape[2]
    tokens, topk = expert_ids.shape
    span = grad_out.shape[1]
    square = groups == 8 and sections == 4
    flat = lambda w: w.reshape(experts * units, features)
    w_gate, w_up, w_down = flat(w_gate), flat(w_up), flat(w_down)
    core = me % 2
    near = jnp.where(core == 0, 2, 4)
    far = 6 - near

    def swap(x, even, odd):
        return lax.ppermute(x, "expert", [(i, i ^ (even, odd)[i % 2]) for i in range(groups)])

    def across(x, by):
        return lax.ppermute(x, "section", [(i, i ^ by) for i in range(sections)])

    if square:
        owners = jnp.stack([me, me ^ 1, me ^ near, me ^ near ^ 1, me ^ 1 ^ far, me ^ far, me ^ 6, me ^ 7])
        moves = (0, 4, 1, 2, 5, 6, 3, 7)
    else:
        owners, moves = jnp.arange(groups), tuple(range(groups))

    piece = grad_out[None, None]
    received = [piece] + [across(piece, i) for i in (1, 2) if i < sections]
    info = jnp.concatenate([expert_ids.T.astype(F32), probs.T], axis=0)[None]
    if square:
        sib0 = swap(piece, 1, 1)
        near0 = [swap(piece, 2, 4), swap(sib0, 2, 4)]
        info = after(info, near0[0])
        for bit in (2, 4, 1):
            info = jnp.concatenate([info, swap(info, bit, bit)], axis=0)
        place = owners ^ me
        place = place // 2 + place % 2 * 4
    else:
        info = lax.all_gather(info, "expert", axis=0, tiled=True)
        place = owners
    at = jnp.concatenate([jnp.stack([z, me * experts]), owners, place]).astype(jnp.int32)
    gated = lambda at: coefficients(at, info, topk, saved_gate, saved_up, slots // groups)
    if square:
        got = [after(x, info) for x in received[1:3]]
        near0 = [after(x, *got) for x in near0]
        pair1 = join(got, [swap(x, 1, 1) for x in got])
        first1 = swap(pair1, 2, 4)
        second0 = swap(near0[0], 4, 2)
        received.append(across(after(piece, pair1), 3))
        coefs = gated(after(at, pair1, *near0))
        got = [after(x, coefs[0]) for x in received[3:]]
        pair2 = join(got, [swap(x, 1, 1) for x in got])
        first1, second0 = after(first1, pair2), after(second0, pair2)
        second1 = swap(first1[:1], 4, 2)
        first2 = swap(after(pair2, first1), 2, 4)
        lot0 = [piece, sib0, *near0, *[swap(x, 1, 1) for x in near0]], [second0, swap(second0, 1, 1)]
        lot1 = [pair1, first1, swap(first1, 1, 1)]
        (most,) = hidden(at, [(None, [(0, lot0[0]), (1, lot1)])], tokens, after(w_down, coefs[0]))
        second1, first2, _ = lax.optimization_barrier((second1, first2, most))
        second2 = swap(first2[:1], 4, 2)
        lot1 = [second1, swap(second1, 1, 1)]
        (few,) = hidden(at, [(None, [(0, lot0[1]), (1, lot1)])], tokens, w_down)
        second2 = after(second2, few)
        lot2 = [pair2, first2, swap(first2, 1, 1)], [second2, swap(second2, 1, 1)]
        parts = [(most, [(3, lot2[0])]), (few, [(3, lot2[1])])]
    else:
        received += [across(piece, i) for i in range(3, sections)]
        coefs = gated(at)
        gather = lambda xs: [lax.all_gather(jnp.concatenate(xs, axis=1), "expert", axis=0, tiled=True)]
        (h,) = hidden(at, [(None, [(0, gather(received[:3]))])], tokens, w_down)
        parts = [(h, [(3, gather(received[3:]))])]
    more = -(-2 * groups * experts * tokens // (16 * span)) * 16
    ag, au, info = hidden(at, parts, tokens, w_down, coefs, experts, moves, more)

    lots = ((3, sections), (2, 3), (1, 2), (0, 1))
    half = groups // 2
    last = [info]
    theirs, kept, sent, parts, firsts = {}, {}, {}, {}, {}

    def run_expand(n, part, counts, other=None):
        a, b = lots[n]
        outs = expand(
            at, a, b - a, part, after(ag, *last), au, w_gate, w_up, sections, tokens, counts,
            info if n == 0 else None, other,
        )
        last[0] = outs[0]
        return outs

    def theirs_step(n):
        theirs[n] = swap(run_expand(n, 1, (half,))[0], 1, 1)

    def mine_step(n):
        alone, two, one = run_expand(n, 0, (1, 2, 1), theirs[n])
        kept[n] = alone, two, swap(one, 4, 2)

    def sent_step(n):
        _, two, one = kept[n]
        last[0] = pass_on(two, after(one, *last))
        sent[n] = swap(last[0], 2, 4)

    def receive_step(n):
        got = after(sent[n], *last)
        sent[n] = got[:1], swap(got[1:], 1, 1)

    def final_step(n):
        extra = (parts[0], firsts[0]) if n == 1 else ()
        x = finish(tokens, after(kept[n][0], *last), *sent[n], *extra)
        last[0] = firsts[n] = x
        parts[n] = across(x, (1, 2, 1)[n]) if n < 3 else x

    if square:
        for step, n in (
            (theirs_step, 0),
            (theirs_step, 1),
            (mine_step, 0),
            (mine_step, 1),
            (sent_step, 0),
            (theirs_step, 2),
            (theirs_step, 3),
            (sent_step, 1),
            (receive_step, 0),
            (mine_step, 2),
            (mine_step, 3),
            (sent_step, 2),
            (final_step, 0),
            (receive_step, 1),
            (sent_step, 3),
            (final_step, 1),
            (receive_step, 2),
            (final_step, 2),
            (receive_step, 3),
            (final_step, 3),
        ):
            step(n)
        parts[1] = after(parts[1], firsts[2], sent[3][1])
        grad_in = add(parts[1][:tokens], parts[2], parts[3])
        router = firsts[1][tokens:].astype(F32) + parts[1][tokens:].astype(F32)
    else:
        terms = []
        for n, (a, b) in enumerate(lots):
            sums = lax.psum_scatter(run_expand(n, 0, (groups,))[0], "expert", scatter_dimension=0, tiled=True)[0]
            if n == 0:
                router = lax.psum(sums[0, tokens:].astype(F32), "section")
            terms += [across(sums[i - a, :tokens], i) if i else sums[0] for i in range(a, b)]
        grad_in = add(*terms)

    count = groups * experts
    router = jnp.sum(router.reshape(-1)[: 2 * count * tokens].reshape(2, count, tokens), axis=0)
    match = expert_ids[None] == jnp.arange(count)[:, None, None]
    grad_probs = jnp.sum(jnp.where(match, router[:, :, None], 0.0), axis=0).astype(BF16)
    return (grad_in, grad_probs)


def solution(mesh):
    placed = (
        P("expert", "section"),
        P("expert", None),
        P("expert", None),
        P("expert", "section", None),
        P("expert", "section", None),
        P("expert", "section", None),
        P("expert", "section", None),
        P("expert", "section", None),
    )
    return jax.shard_map(
        local,
        mesh=mesh,
        in_specs=placed,
        out_specs=(P("expert", "section"), P("expert", None)),
        check_vma=False,
    )
```
